32 devices in a mesh: grp: 4 (over x, core), col: 4 (over z), dev: 2 (over y).
Axes of the slice: x: 2, y: 2, z: 4, core: 2. Of those that a mesh axis runs over, the one named last changes fastest.
Arguments:
- rho_re: float32 [12288, 512], P(('grp', 'col'), 'dev'), may hold values from -0.078125 to 0.078125
- rho_im: float32 [12288, 512], P(('grp', 'col'), 'dev'), may hold values from -0.078125 to 0.078125
- coulomb: float32 [12288], P(('grp', 'col', 'dev')), may hold values from 0.4 to 1.6
- chi_prev: float32 [2, 4, 4, 768, 12288], P(None, None, 'col', 'dev', 'grp'), may hold values from -0.013671875 to 0.013671875
- source: float32 [12288, 128], P(('grp', 'col', 'dev')), may hold values from -6 to 6
- band_v: int32 [512], P('dev'), may hold values from 0 to 127
- band_c: int32 [512], P('dev'), may hold values from 128 to 255
- band_energy: float32 [256], replicated, may hold values from -2 to 2.5, as said below
- band_occ: float32 [256], replicated, may hold values from 0 to 1, as said below
Outputs:
- screened_re: float32 [12288, 128], P(('grp', 'col', 'dev'))
- screened_im: float32 [12288, 128], P(('grp', 'col', 'dev'))
The draws below stay inside these ranges and needn't reach their ends.
Inputs may be any that keep to these rules, and one draw needn't show every extreme that they name: `band_v`: the valence bands are the first 128. `band_energy`: the first 128 bands lie below -0.1, the others above 0.2. `band_occ`: the first 128 bands have occupations of 0.7 or more, the others of 0.3 or less.
All inputs are finite; a program needn't handle non-finite values.
Results may differ from the reference program's by a relative error of at most 0.00013.
Values sent between devices are 32-bit elements; how exact they have to be, the bound alone decides.
No kernel may reach another device: no remote copies, remote signals or barrier semaphores. Data moves between devices by JAX's collectives and lax.ppermute only.
A program may use at most 128 MiB of HBM per device.

```python
import math
import jax
import jax.numpy as jnp
from jax import lax

NG = 12288
NP = 512
NW = 128
NB = 256
ITERS = 2
NV = 128
SLAB = 768
N_GRP = 4
N_COL = 4


def draw_band_energy(key, part):
    first, second = jax.random.split(jax.random.fold_in(key, 11))
    band_index = jnp.arange(NB)
    lower = jax.random.uniform(first, (NB,), jnp.float32, -2.0, -0.1)
    upper = jax.random.uniform(second, (NB,), jnp.float32, 0.2, 2.5)
    return jnp.where(band_index < NV, lower, upper)


def draw_band_occ(key, part):
    first, second = jax.random.split(jax.random.fold_in(key, 23))
    band_index = jnp.arange(NB)
    lower = jax.random.uniform(first, (NB,), jnp.float32, 0.7, 1.0)
    upper = jax.random.uniform(second, (NB,), jnp.float32, 0.0, 0.3)
    return jnp.where(band_index < NV, lower, upper)


def set_ends(drawn, rng, least, high):
    longest = drawn.shape.index(max(drawn.shape))
    spots = []
    for shift in (0, 1):
        where = [jax.random.randint(jax.random.fold_in(rng, axis), (), 0, length) for axis, length in enumerate(drawn.shape)]
        where[longest] = (where[longest] + shift) % drawn.shape[longest]
        spots.append(tuple(where))
    return drawn.at[spots[0]].set(least).at[spots[1]].set(high)


def block_scale(rng, dims, shards, least, high):
    loudness = 1.0
    for position, blocks in shards:
        heights = jax.random.uniform(jax.random.fold_in(jax.random.fold_in(rng, 6), position), (blocks,), jnp.float32, least / len(shards), high / len(shards))
        loudness = loudness * jnp.repeat(jnp.exp(heights), dims[position] // blocks).reshape((-1,) + (1,) * (len(dims) - 1 - position))
    return loudness


def noise(stream_key, extent, deviation, bound, shards=(), held_as=jnp.bfloat16):
    array = deviation * jax.random.normal(stream_key, extent, jnp.float32)
    if shards:
        array = array * block_scale(stream_key, extent, shards, -0.22, 0.18)
    return jnp.clip(array, -bound, bound).astype(held_as)


def setup_inputs(seed: int = 0) -> dict:
    streams_of = jax.random.split(jax.random.key(seed), 10)
    return {
        "rho_re": noise(streams_of[0], (NG, NP), (NG // 2) ** -0.5, 0.078125, ((0, 16), (1, 2)), jnp.float32),
        "rho_im": noise(streams_of[1], (NG, NP), (NG // 2) ** -0.5, 0.078125, ((0, 16), (1, 2)), jnp.float32),
        "coulomb": jnp.clip(jnp.exp(math.log(1.6) - 1.3862944 * jax.random.uniform(streams_of[2], (NG,), jnp.float32) ** block_scale(streams_of[2], (NG,), ((0, 32),), -0.2, 0.2)), 0.4, 1.6),
        "chi_prev": noise(streams_of[3], (2, N_GRP, N_COL, SLAB, NG), (16 * NG) ** -0.5, 0.013671875, ((2, 4), (3, 2), (4, 4)), jnp.float32),
        "source": noise(streams_of[4], (NG, NW), 1.0, 6.0, ((0, 32),), jnp.float32),
        "band_v": set_ends(jax.random.randint(streams_of[5], (NP,), 0, NV), jax.random.fold_in(streams_of[5], 1), 0, NV - 1).astype(jnp.int32),
        "band_c": set_ends(jax.random.randint(streams_of[6], (NP,), NV, NB), jax.random.fold_in(streams_of[6], 1), NV, NB - 1).astype(jnp.int32),
        "band_energy": draw_band_energy(jax.random.fold_in(streams_of[9], 71), 0),
        "band_occ": draw_band_occ(jax.random.fold_in(streams_of[9], 71), 0),
    }


frequency = 0.8
damping = 0.5


def pair_weight(band_v, band_c, band_energy, band_occ):
    delta = band_energy[band_c] - band_energy[band_v]
    filling = band_occ[band_v] - band_occ[band_c]
    return filling * 2.0 * delta / (delta * delta + frequency * frequency)


def contract(left, right):
    return lax.dot_general(left, right, (((0,), (0,)), ((), ())), precision=lax.Precision.HIGHEST, preferred_element_type=jnp.float32)


def matmul(left, right):
    return jnp.dot(left, right, precision=lax.Precision.HIGHEST, preferred_element_type=jnp.float32)


def reference(rho_re, rho_im, coulomb, chi_prev, source, band_v, band_c, band_energy, band_occ):
    weight = pair_weight(band_v, band_c, band_energy, band_occ)
    previous = chi_prev.reshape(2, NG, NG)
    scale = coulomb[:, None]
    real_part = source
    imag_part = jnp.zeros_like(source)
    for sweep in range(ITERS):
        scaled_re = scale * real_part
        scaled_im = scale * imag_part
        image_re = contract(previous[0], scaled_re) - contract(previous[1], scaled_im)
        image_im = contract(previous[0], scaled_im) + contract(previous[1], scaled_re)
        proj_re = contract(rho_re, scaled_re) + contract(rho_im, scaled_im)
        proj_im = contract(rho_re, scaled_im) - contract(rho_im, scaled_re)
        proj_re = weight[:, None] * proj_re
        proj_im = weight[:, None] * proj_im
        image_re = image_re - (matmul(rho_re, proj_re) - matmul(rho_im, proj_im))
        image_im = image_im - (matmul(rho_re, proj_im) + matmul(rho_im, proj_re))
        image_re = scale * image_re
        image_im = scale * image_im
        real_part = real_part + damping * (source + image_re - real_part)
        imag_part = imag_part + damping * (image_im - imag_part)
    return real_part, imag_part
```

```python
import functools

import jax
import jax.numpy as jnp
from jax import lax
from jax.experimental import pallas as pl
from jax.experimental.pallas import tpu as pltpu
from jax.sharding import PartitionSpec as P

ITERS = 2


frequency = 0.8
damping = 0.5
MIB = 1 << 20


def lookup(bands, table):
    band_index = jnp.arange(table.shape[0], dtype=jnp.int32)
    match = bands[None, :] == band_index[:, None]
    return jnp.sum(jnp.where(match, table[:, None], 0.0), axis=0)


def pair_weight(band_v, band_c, band_energy, band_occ):
    delta = lookup(band_c, band_energy) - lookup(band_v, band_energy)
    filling = lookup(band_v, band_occ) - lookup(band_c, band_occ)
    return filling * 2.0 * delta / (delta * delta + frequency * frequency)


def contract(left, right):
    return lax.dot_general(
        left,
        right,
        (((0,), (0,)), ((), ())),
        precision=lax.Precision.HIGHEST,
        preferred_element_type=jnp.float32,
    )


def matmul(left, right):
    return jnp.dot(left, right, precision=lax.Precision.HIGHEST, preferred_element_type=jnp.float32)


def general(rho_re, rho_im, coulomb, chi_prev, source, band_v, band_c, band_energy, band_occ):
    weight = pair_weight(band_v, band_c, band_energy, band_occ)
    slab = rho_re.shape[0]
    width = source.shape[1]
    row_block = chi_prev.shape[4]
    my_cols = chi_prev.shape[1] * chi_prev.shape[3]
    previous = chi_prev.reshape(2, my_cols, row_block)
    scale = coulomb[:, None]
    real_part = source
    imag_part = jnp.zeros_like(source)
    for sweep in range(ITERS):
        scaled = jnp.concatenate([scale * real_part, scale * imag_part], axis=1)
        piece = lax.all_gather(scaled, "grp", axis=0, tiled=True)
        swapped = jnp.concatenate([-piece[:, width:], piece[:, :width]], axis=1)
        total = contract(previous[0], piece) + contract(previous[1], swapped)
        slab_scaled = lax.all_gather(scaled, "dev", axis=0, tiled=True)
        slab_re = slab_scaled[:, :width]
        slab_im = slab_scaled[:, width:]
        proj_re = contract(rho_re, slab_re) + contract(rho_im, slab_im)
        proj_im = contract(rho_re, slab_im) - contract(rho_im, slab_re)
        summed = lax.psum(jnp.concatenate([proj_re, proj_im], axis=1), ("grp", "col"))
        weighted = weight[:, None] * summed
        weighted_re = weighted[:, :width]
        weighted_im = weighted[:, width:]
        added_re = -(matmul(rho_re, weighted_re) - matmul(rho_im, weighted_im))
        added_im = -(matmul(rho_re, weighted_im) + matmul(rho_im, weighted_re))
        offset = lax.axis_index("col") * slab
        current = lax.dynamic_slice(total, (offset, 0), (slab, 2 * width))
        total = lax.dynamic_update_slice(
            total, current + jnp.concatenate([added_re, added_im], axis=1), (offset, 0)
        )
        mine = lax.psum_scatter(total, ("col", "dev"), scatter_dimension=0, tiled=True)
        image_re = scale * mine[:, :width]
        image_im = scale * mine[:, width:]
        real_part = real_part + damping * (source + image_re - real_part)
        imag_part = imag_part + damping * (image_im - imag_part)
    return (real_part, imag_part)


def split(value):
    high = value.astype(jnp.bfloat16)
    return high, (value - high.astype(jnp.float32)).astype(jnp.bfloat16)


def dot(left, right):
    return jnp.dot(left, right, preferred_element_type=jnp.float32)


def dot_nt(left, right):
    return lax.dot_general(
        left, right, (((1,), (1,)), ((), ())), preferred_element_type=jnp.float32
    )


def dot3(stacked, rows, right, product=dot):
    high, low = split(right)
    both = product(stacked, high)
    return both[:rows] + both[rows:] + product(stacked[:rows], low)


def stack(value):
    high, low = split(value)
    return jnp.concatenate([high, low], axis=0)


def call(kernel, name, scalars, grid, in_specs, out_specs, out_shape, scratch, cost, *operands):
    return pl.pallas_call(
        kernel,
        name=name,
        grid_spec=pltpu.PrefetchScalarGridSpec(
            num_scalar_prefetch=1,
            grid=grid,
            in_specs=in_specs,
            out_specs=out_specs,
            scratch_shapes=scratch,
        ),
        out_shape=out_shape,
        cost_estimate=pl.CostEstimate(flops=cost[0], bytes_accessed=cost[1], transcendentals=0),
        compiler_params=pltpu.CompilerParams(
            vmem_limit_bytes=36 * MIB, dimension_semantics=("arbitrary",) * len(grid)
        ),
    )(scalars, *operands)


def whole(*shape):
    return pl.BlockSpec(shape, lambda *_: (0,) * len(shape))


def shaped(*shape):
    return jax.ShapeDtypeStruct(shape, jnp.float32)


def apply_block(panel, rows, width, chi, out, start=None):
    depth = chi.shape[1] * chi.shape[2]
    part_re = dot3(panel[...], rows, chi[0].reshape(depth, chi.shape[3]))
    part_im = dot3(panel[...], rows, chi[1].reshape(depth, chi.shape[3]))
    if rows == 2 * width:
        image_re = part_re[:width] - part_im[width:]
        image_im = part_re[width:] + part_im[:width]
    else:
        image_re = part_re
        image_im = part_im
    if start is not None:
        image_re = start[:width] + image_re
        image_im = start[width:] + image_im
    out[:width] = image_re
    out[width:] = image_im


def fill_panel(panel, core, near, far):
    rows, half = near.shape
    for piece, place in ((near, core), (far, 1 - core)):
        high, low = split(piece[...])
        at = pl.ds(pl.multiple_of(place * half, half), half)
        panel[:rows, at] = high
        panel[rows:, at] = low


def begin_kernel(scalars, source, coulomb, bare, scaled):
    turned = source[...].T
    bare[...] = turned
    scaled[...] = turned * coulomb[...]


def local_kernel(width, scalars, near, far, chi, out, panel):
    @pl.when(pl.program_id(0) == 0)
    def _():
        fill_panel(panel, scalars[1], near, far)

    apply_block(panel, near.shape[0], width, chi, out)


def half_kernel(width, scalars, near, far, chi, start, *rest):
    *outs, panel = rest
    step = pl.program_id(0)

    @pl.when(step == 0)
    def _():
        fill_panel(panel, scalars[1], near, far)

    for index, out in enumerate(outs):

        @pl.when(step == index)
        def _():
            apply_block(panel, near.shape[0], width, chi, out, start)


def slab_kernel(width, scalars, near, far, chi, start, *rest):
    *outs, panel, full = rest
    step = pl.program_id(0)
    half = near.shape[1]

    @pl.when(step == 0)
    def _():
        fill_panel(panel, scalars[1], near, far)

    apply_block(panel, near.shape[0], width, chi, full, start)
    for index in range(len(outs) // 2):

        @pl.when(step == index)
        def _():
            for place, out in zip((1 - scalars[3], scalars[3]), outs[2 * index : 2 * index + 2]):
                out[...] = full[:, pl.ds(pl.multiple_of(place * half, half), half)]


def project_kernel(width, scalars, near, far, rho_re, rho_im, keep, send, full):
    rows, half = near.shape
    dev, core = scalars[3], scalars[1]
    total_re = total_im = None
    for piece, place in ((near, dev), (far, 1 - dev)):
        at = pl.ds(pl.multiple_of(place * half, half), half)
        panel = stack(piece[...])
        by_re = dot3(panel, rows, rho_re[at])
        by_im = dot3(panel, rows, rho_im[at])
        total_re = by_re if total_re is None else total_re + by_re
        total_im = by_im if total_im is None else total_im + by_im
    if rows == 2 * width:
        full[:width] = total_re[:width] + total_im[width:]
        full[width:] = total_re[width:] - total_im[:width]
    else:
        full[:width] = total_re
        full[width:] = -total_im
    keep[...] = full[pl.ds(pl.multiple_of(core * width, width), width)]
    send[...] = full[pl.ds(pl.multiple_of((1 - core) * width, width), width)]


def spread_kernel(width, scalars, near, far, weight, rho_re, rho_im, first, second, first_out, second_out, full):
    half = first.shape[1]
    dev, core = scalars[3], scalars[1]
    full[pl.ds(pl.multiple_of(core * width, width), width)] = weight[...] * near[...]
    full[pl.ds(pl.multiple_of((1 - core) * width, width), width)] = weight[...] * far[...]
    panel = stack(full[...])
    for place, given, out in ((1 - dev, first, first_out), (dev, second, second_out)):
        at = pl.ds(pl.multiple_of(place * half, half), half)
        by_re = dot3(panel, 2 * width, rho_re[at], dot_nt)
        by_im = dot3(panel, 2 * width, rho_im[at], dot_nt)
        out[:width] = given[:width] - (by_re[:width] - by_im[width:])
        out[width:] = given[width:] - (by_re[width:] + by_im[:width])


def end_kernel(width, scalars, own, by_dev, by_near, by_far, iterate, bare, coulomb, out_re, out_im):
    image = coulomb[...] * (own[...] + by_dev[...] + by_near[...] + by_far[...])
    real_part = iterate[:width]
    imag_part = iterate[width:]
    real_part = real_part + damping * (bare[...] + image[:width] - real_part)
    imag_part = imag_part + damping * (image[width:] - imag_part)
    out_re[...] = real_part.T
    out_im[...] = imag_part.T


def exchange(value, axis, flip):
    size = lax.axis_size(axis)
    return lax.ppermute(value, axis, [(i, i ^ flip) for i in range(size)])


def exchanged(rho_re, rho_im, coulomb, chi_prev, source, band_v, band_c, band_energy, band_occ):
    weight = pair_weight(band_v, band_c, band_energy, band_occ)[None, :]
    half, width = source.shape
    pairs = rho_re.shape[1]
    slab = 2 * half
    panel_rows = 2 * width
    parts = chi_prev.shape[0]
    row_block = chi_prev.shape[4]
    n_slab = row_block // slab
    last = n_slab - 1
    grp = lax.axis_index("grp")
    scalars = jnp.stack([grp // 2, grp % 2, lax.axis_index("col"), lax.axis_index("dev")]).astype(jnp.int32)
    scale = coulomb[None, :]

    bare, scaled = call(
        begin_kernel, "begin", scalars, (1,),
        [whole(half, width), whole(1, half)],
        [whole(width, half)] * 2,
        [shaped(width, half)] * 2,
        [], (0, 12 * half * width),
        source, scale,
    )

    def chi_block(columns, pair, place):
        return pl.BlockSpec((parts, 2, None, half, columns), lambda i, s: (0, pair(s), 0, 0, place(i, s)))

    def products(blocks, rows, columns):
        flops = 3 * 2 * 2 * blocks * rows * slab * columns
        return flops, 4 * blocks * columns * (parts * slab + panel_rows)

    here = lambda s: s[0]
    there = lambda s: 1 - s[0]

    def image(scaled):
        rows = scaled.shape[0]
        from_x = exchange(scaled, "grp", 2)
        from_core = exchange(scaled, "grp", 1)
        from_dev = exchange(scaled, "dev", 1)
        panel = pltpu.VMEM((2 * rows, slab), jnp.bfloat16)
        pieces = [whole(rows, half)] * 2

        start = call(
            functools.partial(local_kernel, width), "near_half", scalars, (n_slab,),
            pieces + [chi_block(slab, here, lambda i, s: s[2] ^ (last - i))],
            pl.BlockSpec((None, panel_rows, slab), lambda i, s: (i, 0, 0)),
            shaped(n_slab, panel_rows, slab),
            [panel], products(n_slab, rows, slab),
            scaled, from_core, chi_prev,
        )

        keep, send = call(
            functools.partial(project_kernel, width), "project", scalars, (1,),
            pieces + [whole(slab, pairs)] * 2,
            [whole(width, pairs)] * 2,
            [shaped(width, pairs)] * 2,
            [pltpu.VMEM((panel_rows, pairs), jnp.float32)],
            (3 * 4 * rows * slab * pairs, 8 * slab * pairs),
            scaled, from_dev, rho_re, rho_im,
        )
        total = keep + exchange(send, "grp", 1)
        total = total + exchange(total, "grp", 2)
        total = total + exchange(total, "col", 1)
        total = total + exchange(total, "col", 2)
        other = exchange(total, "grp", 1)

        from_x_core = exchange(from_x, "grp", 1)

        def by_halves(places):
            def at(i, s):
                where = [2 * (s[2] ^ j) + (1 - s[3] if sent else s[3]) for j, sent in places]
                found = where[-1]
                for index in range(len(places) - 2, -1, -1):
                    found = jnp.where(i == index, where[index], found)
                return found

            def begun(i, s):
                row, col = last - places[-1][0], (1 - s[3] if places[-1][1] else s[3])
                for index in range(len(places) - 2, -1, -1):
                    j, sent = places[index]
                    row = jnp.where(i == index, last - j, row)
                    col = jnp.where(i == index, 1 - s[3] if sent else s[3], col)
                return row, 0, col

            return call(
                functools.partial(half_kernel, width), f"far_half_{len(places)}", scalars, (len(places),),
                pieces + [chi_block(half, there, at), pl.BlockSpec((None, panel_rows, half), begun)],
                [whole(panel_rows, half)] * len(places),
                [shaped(panel_rows, half)] * len(places),
                [panel], products(len(places), rows, half),
                from_x, from_x_core, chi_prev, start,
            )

        def by_slabs(first, count):
            return call(
                functools.partial(slab_kernel, width), f"far_slab_{count}", scalars, (count,),
                pieces + [
                    chi_block(slab, there, lambda i, s: s[2] ^ (first - i)),
                    pl.BlockSpec((None, panel_rows, slab), lambda i, s: (last - first + i, 0, 0)),
                ],
                [whole(panel_rows, half)] * (2 * count),
                [shaped(panel_rows, half)] * (2 * count),
                [panel, pltpu.VMEM((panel_rows, slab), jnp.float32)],
                products(count, rows, slab),
                from_x, from_x_core, chi_prev, start,
            )

        (send3,) = by_halves([(3, True)])
        got3 = exchange(send3, "dev", 1)
        send2, keep2, keep3 = by_halves([(2, True), (2, False), (3, False)])
        got2 = exchange(send2, "dev", 1)
        send1, keep1, send0, keep0 = by_slabs(1, 2)
        got1 = exchange(send1, "dev", 1)
        send0, keep0 = call(
            functools.partial(spread_kernel, width), "spread", scalars, (1,),
            [whole(width, pairs)] * 2 + [whole(1, pairs)] + [whole(slab, pairs)] * 2 + [whole(panel_rows, half)] * 2,
            [whole(panel_rows, half)] * 2,
            [shaped(panel_rows, half)] * 2,
            [pltpu.VMEM((panel_rows, pairs), jnp.float32)],
            (3 * 4 * panel_rows * slab * pairs, 8 * slab * pairs),
            total, other, weight, rho_re, rho_im, send0, keep0,
        )
        got0 = exchange(send0, "dev", 1)
        across = exchange(keep3 + got3, "col", 1)
        far = exchange(keep2 + got2 + across, "col", 2)
        near = exchange(keep1 + got1, "col", 1)
        return keep0, got0, near, far

    own, by_dev, by_near, by_far = image(scaled)
    pulled = scale * (own + by_dev + by_near + by_far)
    real_part = bare + damping * (bare + pulled[:width] - bare)
    imag_part = damping * pulled[width:]
    iterate = jnp.concatenate([real_part, imag_part], axis=0)
    for sweep in range(1, ITERS):
        own, by_dev, by_near, by_far = image(scale * iterate)
    return call(
        functools.partial(end_kernel, width), "end", scalars, (1,),
        [whole(panel_rows, half)] * 5 + [whole(width, half), whole(1, half)],
        [whole(half, width)] * 2,
        [shaped(half, width)] * 2,
        [], (0, 4 * 8 * half * panel_rows),
        own, by_dev, by_near, by_far, iterate, bare, scale,
    )


def solution(mesh):
    placed = (
        P(("grp", "col"), "dev"),
        P(("grp", "col"), "dev"),
        P(("grp", "col", "dev")),
        P(None, None, "col", "dev", "grp"),
        P(("grp", "col", "dev"), None),
        P("dev"),
        P("dev"),
        P(),
        P(),
    )

    def shards(*blocks):
        half, width = blocks[4].shape
        pairs = blocks[0].shape[1]
        paired = mesh.shape["grp"] == 4 and mesh.shape["col"] == 4 and mesh.shape["dev"] == 2
        tiled = half % 128 == 0 and width % 128 == 0 and pairs % 128 == 0
        return (exchanged if paired and tiled and ITERS == 2 else general)(*blocks)

    return jax.shard_map(
        shards,
        mesh=mesh,
        in_specs=placed,
        out_specs=(P(("grp", "col", "dev"), None), P(("grp", "col", "dev"), None)),
        check_vma=False,
    )
```

```python
import functools

import jax
import jax.numpy as jnp
from jax import lax
from jax.experimental import pallas as pl
from jax.experimental.pallas import tpu as pltpu
from jax.sharding import PartitionSpec as P

ITERS = 2


frequency = 0.8
damping = 0.5
MIB = 1 << 20
DEPTH = 4
LIMIT = 8
HURRY = 64
AHEAD = 3


def lookup(bands, table):
    band_index = jnp.arange(table.shape[0], dtype=jnp.int32)
    match = bands[None, :] == band_index[:, None]
    return jnp.sum(jnp.where(match, table[:, None], 0.0), axis=0)


def pair_weight(band_v, band_c, band_energy, band_occ):
    delta = lookup(band_c, band_energy) - lookup(band_v, band_energy)
    filling = lookup(band_v, band_occ) - lookup(band_c, band_occ)
    return filling * 2.0 * delta / (delta * delta + frequency * frequency)


def contract(left, right):
    return lax.dot_general(
        left,
        right,
        (((0,), (0,)), ((), ())),
        precision=lax.Precision.HIGHEST,
        preferred_element_type=jnp.float32,
    )


def matmul(left, right):
    return jnp.dot(left, right, precision=lax.Precision.HIGHEST, preferred_element_type=jnp.float32)


def general(rho_re, rho_im, coulomb, chi_prev, source, band_v, band_c, band_energy, band_occ):
    weight = pair_weight(band_v, band_c, band_energy, band_occ)
    slab = rho_re.shape[0]
    width = source.shape[1]
    row_block = chi_prev.shape[4]
    my_cols = chi_prev.shape[1] * chi_prev.shape[3]
    previous = chi_prev.reshape(2, my_cols, row_block)
    scale = coulomb[:, None]
    real_part = source
    imag_part = jnp.zeros_like(source)
    for sweep in range(ITERS):
        scaled = jnp.concatenate([scale * real_part, scale * imag_part], axis=1)
        piece = lax.all_gather(scaled, "grp", axis=0, tiled=True)
        swapped = jnp.concatenate([-piece[:, width:], piece[:, :width]], axis=1)
        total = contract(previous[0], piece) + contract(previous[1], swapped)
        slab_scaled = lax.all_gather(scaled, "dev", axis=0, tiled=True)
        slab_re = slab_scaled[:, :width]
        slab_im = slab_scaled[:, width:]
        proj_re = contract(rho_re, slab_re) + contract(rho_im, slab_im)
        proj_im = contract(rho_re, slab_im) - contract(rho_im, slab_re)
        summed = lax.psum(jnp.concatenate([proj_re, proj_im], axis=1), ("grp", "col"))
        weighted = weight[:, None] * summed
        weighted_re = weighted[:, :width]
        weighted_im = weighted[:, width:]
        added_re = -(matmul(rho_re, weighted_re) - matmul(rho_im, weighted_im))
        added_im = -(matmul(rho_re, weighted_im) + matmul(rho_im, weighted_re))
        offset = lax.axis_index("col") * slab
        current = lax.dynamic_slice(total, (offset, 0), (slab, 2 * width))
        total = lax.dynamic_update_slice(
            total, current + jnp.concatenate([added_re, added_im], axis=1), (offset, 0)
        )
        mine = lax.psum_scatter(total, ("col", "dev"), scatter_dimension=0, tiled=True)
        image_re = scale * mine[:, :width]
        image_im = scale * mine[:, width:]
        real_part = real_part + damping * (source + image_re - real_part)
        imag_part = imag_part + damping * (image_im - imag_part)
    return (real_part, imag_part)


def split(value):
    high = value.astype(jnp.bfloat16)
    return high, (value - high.astype(jnp.float32)).astype(jnp.bfloat16)


def dot(left, right):
    return jnp.dot(left, right, preferred_element_type=jnp.float32)


def dot_nt(left, right):
    return lax.dot_general(
        left, right, (((1,), (1,)), ((), ())), preferred_element_type=jnp.float32
    )


def dot3(stacked, rows, right, product=dot):
    high, low = split(right)
    both = product(stacked, high)
    return both[:rows] + both[rows:] + product(stacked[:rows], low)


def stack(value):
    high, low = split(value)
    return jnp.concatenate([high, low], axis=0)


def small(kernel, name, scalars, out_shape, scratch, cost, *operands, chi=None, limit=LIMIT):
    vmem = pl.BlockSpec(memory_space=pltpu.VMEM)
    in_specs = [pl.BlockSpec(memory_space=pltpu.SMEM)] + [vmem] * len(operands)
    if chi is not None:
        in_specs.append(pl.BlockSpec(memory_space=pl.ANY))
        operands += (chi,)
    return pl.pallas_call(
        kernel,
        name=name,
        in_specs=in_specs,
        out_specs=[vmem] * len(out_shape),
        out_shape=out_shape,
        scratch_shapes=scratch,
        cost_estimate=pl.CostEstimate(flops=cost[0] // HURRY, bytes_accessed=cost[1] // HURRY, transcendentals=0),
        compiler_params=pltpu.CompilerParams(vmem_limit_bytes=limit * MIB),
    )(scalars, *operands)


def shaped(*shape):
    return jax.ShapeDtypeStruct(shape, jnp.float32)


def product3(stacked, rows, high, low):
    both = dot(stacked, high)
    return both[:rows] + both[rows:] + dot(stacked[:rows], low)


def fill_panel(panel, core, near, far, width):
    rows, half = near.shape
    for piece, place in ((near, core), (far, 1 - core)):
        at = pl.ds(pl.multiple_of(place * half, half), half)
        high, low = split(piece[...])
        panel[0, :rows, at] = high
        panel[0, rows:, at] = low
        if rows == 2 * width:
            panel[1, :width, at] = -high[width:]
            panel[1, width:rows, at] = high[:width]
            panel[1, rows : rows + width, at] = -low[width:]
            panel[1, rows + width :, at] = low[:width]


def add_product(total, width, panel, part, block, first):
    if panel.shape[0] == 2:
        rows, stacked, at = 2 * width, panel[part], slice(None)
    else:
        rows, stacked, at = width, panel[0], slice(part * width, (part + 1) * width)
    product = product3(stacked, rows, *split(block))
    total[at] = product if first else total[at] + product


def fetch(scalars, chi, targets, sems, jobs):
    slab = targets[0].shape[-1]
    queue = []
    for (j, far), target in zip(jobs, targets):
        pair = 1 - scalars[0] if far else scalars[0]
        at = pl.ds(pl.multiple_of((scalars[2] ^ j) * slab, slab), slab)
        for part in range(2):
            source = chi.at[part, pl.ds(2 * pair, 2), 0, :, at]
            queue.append(pltpu.make_async_copy(source, target.at[part], sems.at[len(queue)]))
    for copy in queue[:DEPTH]:
        copy.start()

    def arrived(index):
        queue[index].wait()
        if index + DEPTH < len(queue):
            queue[index + DEPTH].start()

    return arrived


def begin_kernel(scalars, source, coulomb, bare, scaled):
    turned = source[...].T
    bare[...] = turned
    scaled[...] = turned * coulomb[...]


def each_block(count, chi, buffers, sems, place, use):
    slots, slab = buffers.shape[0], buffers.shape[-1]

    def copy(t):
        part, pair, row = place(t)
        at = pl.ds(pl.multiple_of(row * slab, slab), slab)
        slot = lax.rem(t, slots)
        return pltpu.make_async_copy(chi.at[part, pl.ds(2 * pair, 2), 0, :, at], buffers.at[slot], sems.at[slot])

    def step(t, carry):
        copy(t).wait()

        @pl.when((t == 0) & (count > 1))
        def _():
            copy(t + 1).start()

        @pl.when(t + 2 < count)
        def _():
            copy(t + 2).start()

        use(t, buffers[lax.rem(t, slots)].reshape(slab, slab))
        return carry

    return copy, step


def first_kernel(width, jobs, scalars, near, far, chi, out, *rest):
    *blocks, panel, sems = rest
    slab = 2 * near.shape[1]
    arrived = fetch(scalars, chi, blocks, sems, jobs)
    fill_panel(panel, scalars[1], near, far, width)
    for part in range(2):
        arrived(part)
        first = part == 0 or panel.shape[0] == 1
        add_product(out.at[0], width, panel, part, blocks[0][part].reshape(slab, slab), first)
    for index in range(2, 2 * len(jobs)):
        arrived(index)


def near_kernel(width, scalars, near, far, *rest):
    *blocks, out, panel = rest
    slab = 2 * near.shape[1]
    fill_panel(panel, scalars[1], near, far, width)
    for index, block in enumerate(blocks):
        for part in range(2):
            first = part == 0 or panel.shape[0] == 1
            add_product(out.at[index], width, panel, part, block[part].reshape(slab, slab), first)


def halves_out(scalars, full, send, keep):
    half = send.shape[1]
    for place, out in ((1 - scalars[3], send), (scalars[3], keep)):
        out[...] = full[:, pl.ds(pl.multiple_of(place * half, half), half)]


def far_kernel(width, begun, scalars, near, far, start, block, send, keep, panel, full):
    slab = 2 * near.shape[1]
    full[...] = start[begun]
    fill_panel(panel, scalars[1], near, far, width)
    for part in range(2):
        add_product(full, width, panel, part, block[part].reshape(slab, slab), False)
    halves_out(scalars, full, send, keep)


def held_kernel(width, scalars, near, near_far, far, far_far, near_block, far_block, send, keep, panel, full):
    slab = 2 * near.shape[1]
    for side, pieces in enumerate(((near, near_far), (far, far_far))):
        fill_panel(panel.at[side], scalars[1], *pieces, width)
    for side, block in enumerate((near_block, far_block)):
        for part in range(2):
            first = side == 0 and (part == 0 or panel.shape[1] == 1)
            add_product(full, width, panel.at[side], part, block[part].reshape(slab, slab), first)
    halves_out(scalars, full, send, keep)


def both_kernel(width, jobs, scalars, near, near_far, far, far_far, chi, *rest):
    count = len(jobs) // 2
    outs, blocks, (panel, full, sems) = rest[: 2 * count], rest[2 * count : 4 * count], rest[4 * count :]
    slab = 2 * near.shape[1]
    arrived = fetch(scalars, chi, blocks, sems, jobs)
    fill_panel(panel.at[0], scalars[1], near, near_far, width)
    fill_panel(panel.at[1], scalars[1], far, far_far, width)
    for index, block in enumerate(blocks):
        side = index % 2
        for part in range(2):
            arrived(2 * index + part)
            first = side == 0 and (part == 0 or panel.shape[1] == 1)
            add_product(full, width, panel.at[side], part, block[part].reshape(slab, slab), first)
        if side == 1:
            halves_out(scalars, full, outs[index - 1], outs[index])


def project_kernel(width, scalars, near, far, rho_re, rho_im, keep, send, full):
    rows, half = near.shape
    dev, core = scalars[3], scalars[1]
    total_re = total_im = None
    for piece, place in ((near, dev), (far, 1 - dev)):
        at = pl.ds(pl.multiple_of(place * half, half), half)
        panel = stack(piece[...])
        by_re = dot3(panel, rows, rho_re[at])
        by_im = dot3(panel, rows, rho_im[at])
        total_re = by_re if total_re is None else total_re + by_re
        total_im = by_im if total_im is None else total_im + by_im
    if rows == 2 * width:
        full[:width] = total_re[:width] + total_im[width:]
        full[width:] = total_re[width:] - total_im[:width]
    else:
        full[:width] = total_re
        full[width:] = -total_im
    keep[...] = full[pl.ds(pl.multiple_of(core * width, width), width)]
    send[...] = full[pl.ds(pl.multiple_of((1 - core) * width, width), width)]


def spread_kernel(width, scalars, near, far, weight, rho_re, rho_im, first, second, first_out, second_out, full):
    half = first.shape[1]
    dev, core = scalars[3], scalars[1]
    full[pl.ds(pl.multiple_of(core * width, width), width)] = weight[...] * near[...]
    full[pl.ds(pl.multiple_of((1 - core) * width, width), width)] = weight[...] * far[...]
    panel = stack(full[...])
    for place, given, out in ((1 - dev, first, first_out), (dev, second, second_out)):
        at = pl.ds(pl.multiple_of(place * half, half), half)
        by_re = dot3(panel, 2 * width, rho_re[at], dot_nt)
        by_im = dot3(panel, 2 * width, rho_im[at], dot_nt)
        out[:width] = given[:width] - (by_re[:width] - by_im[width:])
        out[width:] = given[width:] - (by_re[width:] + by_im[:width])


def end_kernel(width, scalars, own, by_dev, by_near, by_far, iterate, bare, coulomb, out_re, out_im):
    image = coulomb[...] * (own[...] + by_dev[...] + by_near[...] + by_far[...])
    real_part = iterate[:width]
    imag_part = iterate[width:]
    real_part = real_part + damping * (bare[...] + image[:width] - real_part)
    imag_part = imag_part + damping * (image[width:] - imag_part)
    out_re[...] = real_part.T
    out_im[...] = imag_part.T


def after(value, *earlier):
    return lax.optimization_barrier((value, *earlier))[0]


def exchange(value, axis, flip):
    size = lax.axis_size(axis)
    return lax.ppermute(value, axis, [(i, i ^ flip) for i in range(size)])


def exchanged(rho_re, rho_im, coulomb, chi_prev, source, band_v, band_c, band_energy, band_occ):
    weight = pair_weight(band_v, band_c, band_energy, band_occ)[None, :]
    half, width = source.shape
    pairs = rho_re.shape[1]
    slab = 2 * half
    panel_rows = 2 * width
    parts = chi_prev.shape[0]
    row_block = chi_prev.shape[4]
    n_slab = row_block // slab
    last = n_slab - 1
    grp = lax.axis_index("grp")
    scalars = jnp.stack([grp // 2, grp % 2, lax.axis_index("col"), lax.axis_index("dev")]).astype(jnp.int32)
    scale = coulomb[None, :]

    bare, scaled = small(
        begin_kernel, "begin", scalars, [shaped(width, half)] * 2, [], (0, 12 * half * width), source, scale
    )

    def products(blocks, rows):
        flops = 3 * 2 * 2 * blocks * rows * slab * slab
        return flops, 4 * blocks * slab * (parts * slab + panel_rows)

    block_shape = (parts, 2, half, slab)

    def image(scaled, blocks):
        rows = scaled.shape[0]
        from_x = exchange(scaled, "grp", 2)
        from_core = exchange(scaled, "grp", 1)
        from_dev = exchange(scaled, "dev", 1)
        panel_shape = (rows // width, 2 * rows, slab)
        panel = pltpu.VMEM(panel_shape, jnp.bfloat16)
        full = pltpu.VMEM((panel_rows, slab), jnp.float32)
        fresh = not blocks

        if fresh:
            jobs = [(last, False), (last, True)]
            start, *brought = small(
                functools.partial(first_kernel, width, jobs), "first_near", scalars,
                [shaped(1, panel_rows, slab)] + [shaped(*block_shape)] * 2,
                [panel, pltpu.SemaphoreType.DMA((4,))], products(1, rows), scaled, from_core, chi=chi_prev,
            )
            blocks.update(zip(jobs, brought))
        else:
            (start,) = small(
                functools.partial(near_kernel, width), "near_half", scalars, [shaped(AHEAD, panel_rows, slab)],
                [panel], products(AHEAD, rows), scaled, from_core, *[blocks[last - i, False] for i in range(AHEAD)],
            )

        from_x = after(from_x, start)
        from_x_core = exchange(from_x, "grp", 1)
        def far_slab(j, *earlier):
            return small(
                functools.partial(far_kernel, width, last - j), f"far_slab_{j}", scalars,
                [shaped(panel_rows, half)] * 2, [panel, full], products(1, rows),
                from_x, after(from_x_core, *earlier), start, blocks[j, True],
            )

        def held_slab(j, *earlier):
            return small(
                functools.partial(held_kernel, width), f"held_slab_{j}", scalars,
                [shaped(panel_rows, half)] * 2, [pltpu.VMEM((2, *panel_shape), jnp.bfloat16), full],
                products(2, rows),
                scaled, from_core, from_x, after(from_x_core, *earlier), blocks[j, False], blocks[j, True],
            )

        def both_slabs(*slabs, earlier):
            count = len(slabs)
            jobs = [(j, far) for j in slabs for far in (False, True)]
            outs = small(
                functools.partial(both_kernel, width, jobs), f"both_slabs_{count}", scalars,
                [shaped(panel_rows, half)] * (2 * count) + [shaped(*block_shape)] * (2 * count),
                [pltpu.VMEM((2, *panel_shape), jnp.bfloat16), full, pltpu.SemaphoreType.DMA((4 * count,))],
                products(2 * count, rows), scaled, from_core, from_x, after(from_x_core, *earlier), chi=chi_prev,
            )
            blocks.update(zip(jobs, outs[2 * count :]))
            return outs[: 2 * count]

        def slab_of(j, *earlier):
            if fresh:
                return both_slabs(j, earlier=earlier)
            return (far_slab if last - j < AHEAD else held_slab)(j, *earlier)

        send3, keep3 = far_slab(3, start, from_dev)
        got3 = exchange(send3, "dev", 1)
        keep, send = small(
            functools.partial(project_kernel, width), "project", scalars, [shaped(width, pairs)] * 2,
            [pltpu.VMEM((panel_rows, pairs), jnp.float32)],
            (3 * 4 * rows * slab * pairs, 8 * slab * pairs),
            scaled, after(from_dev, start, *(() if fresh else (send3,))), rho_re, rho_im,
        )
        total = keep + exchange(after(send, send3), "grp", 1)
        from_z = exchange(total, "grp", 2)
        send2, keep2 = slab_of(2, send3, keep)
        got2 = exchange(send2, "dev", 1)
        total = total + after(from_z, send2)
        from_z = exchange(total, "col", 1)
        sum3 = keep3 + got3
        across = exchange(sum3, "col", 1)
        send1, keep1 = slab_of(1, send2, total, sum3)
        got1 = exchange(send1, "dev", 1)
        total = total + after(from_z, send1)
        from_z = exchange(total, "col", 2)
        sum2 = keep2 + got2 + across
        far = exchange(sum2, "col", 2)
        send0, keep0 = slab_of(0, send1, total, sum2)
        total = total + after(from_z, send0)
        other = exchange(total, "grp", 1)
        sum1 = keep1 + got1
        near = exchange(sum1, "col", 1)
        send0, keep0 = small(
            functools.partial(spread_kernel, width), "spread", scalars, [shaped(panel_rows, half)] * 2,
            [pltpu.VMEM((panel_rows, pairs), jnp.float32)],
            (3 * 4 * panel_rows * slab * pairs, 8 * slab * pairs),
            total, after(other, sum1), weight, rho_re, rho_im, send0, keep0,
        )
        got0 = exchange(send0, "dev", 1)
        return keep0, got0, near, far

    blocks = {}
    own, by_dev, by_near, by_far = image(scaled, blocks)
    pulled = scale * (own + by_dev + by_near + by_far)
    real_part = bare + damping * (bare + pulled[:width] - bare)
    imag_part = damping * pulled[width:]
    iterate = jnp.concatenate([real_part, imag_part], axis=0)
    for sweep in range(1, ITERS):
        own, by_dev, by_near, by_far = image(scale * iterate, blocks)
    return small(
        functools.partial(end_kernel, width), "end", scalars, [shaped(half, width)] * 2,
        [], (0, 4 * 8 * half * panel_rows),
        own, by_dev, by_near, by_far, iterate, bare, scale,
    )


def solution(mesh):
    placed = (
        P(("grp", "col"), "dev"),
        P(("grp", "col"), "dev"),
        P(("grp", "col", "dev")),
        P(None, None, "col", "dev", "grp"),
        P(("grp", "col", "dev"), None),
        P("dev"),
        P("dev"),
        P(),
        P(),
    )

    def shards(*blocks):
        half, width = blocks[4].shape
        pairs = blocks[0].shape[1]
        paired = mesh.shape["grp"] == 4 and mesh.shape["col"] == 4 and mesh.shape["dev"] == 2
        tiled = half % 128 == 0 and width % 128 == 0 and pairs % 128 == 0
        return (exchanged if paired and tiled and ITERS == 2 else general)(*blocks)

    return jax.shard_map(
        shards,
        mesh=mesh,
        in_specs=placed,
        out_specs=(P(("grp", "col", "dev"), None), P(("grp", "col", "dev"), None)),
        check_vma=False,
    )
```

```python
import functools

import jax
import jax.numpy as jnp
from jax import lax
from jax.experimental import pallas as pl
from jax.experimental.pallas import tpu as pltpu
from jax.sharding import PartitionSpec as P

ITERS = 2


frequency = 0.8
damping = 0.5
MIB = 1 << 20
DEPTH = 4
LIMIT = 8
AHEAD = 3


def lookup(bands, table):
    band_index = jnp.arange(table.shape[0], dtype=jnp.int32)
    match = bands[None, :] == band_index[:, None]
    return jnp.sum(jnp.where(match, table[:, None], 0.0), axis=0)


def pair_weight(band_v, band_c, band_energy, band_occ):
    delta = lookup(band_c, band_energy) - lookup(band_v, band_energy)
    filling = lookup(band_v, band_occ) - lookup(band_c, band_occ)
    return filling * 2.0 * delta / (delta * delta + frequency * frequency)


def contract(left, right):
    return lax.dot_general(
        left,
        right,
        (((0,), (0,)), ((), ())),
        precision=lax.Precision.HIGHEST,
        preferred_element_type=jnp.float32,
    )


def matmul(left, right):
    return jnp.dot(left, right, precision=lax.Precision.HIGHEST, preferred_element_type=jnp.float32)


def general(rho_re, rho_im, coulomb, chi_prev, source, band_v, band_c, band_energy, band_occ):
    weight = pair_weight(band_v, band_c, band_energy, band_occ)
    slab = rho_re.shape[0]
    width = source.shape[1]
    row_block = chi_prev.shape[4]
    my_cols = chi_prev.shape[1] * chi_prev.shape[3]
    previous = chi_prev.reshape(2, my_cols, row_block)
    scale = coulomb[:, None]
    real_part = source
    imag_part = jnp.zeros_like(source)
    for sweep in range(ITERS):
        scaled = jnp.concatenate([scale * real_part, scale * imag_part], axis=1)
        piece = lax.all_gather(scaled, "grp", axis=0, tiled=True)
        swapped = jnp.concatenate([-piece[:, width:], piece[:, :width]], axis=1)
        total = contract(previous[0], piece) + contract(previous[1], swapped)
        slab_scaled = lax.all_gather(scaled, "dev", axis=0, tiled=True)
        slab_re = slab_scaled[:, :width]
        slab_im = slab_scaled[:, width:]
        proj_re = contract(rho_re, slab_re) + contract(rho_im, slab_im)
        proj_im = contract(rho_re, slab_im) - contract(rho_im, slab_re)
        summed = lax.psum(jnp.concatenate([proj_re, proj_im], axis=1), ("grp", "col"))
        weighted = weight[:, None] * summed
        weighted_re = weighted[:, :width]
        weighted_im = weighted[:, width:]
        added_re = -(matmul(rho_re, weighted_re) - matmul(rho_im, weighted_im))
        added_im = -(matmul(rho_re, weighted_im) + matmul(rho_im, weighted_re))
        offset = lax.axis_index("col") * slab
        current = lax.dynamic_slice(total, (offset, 0), (slab, 2 * width))
        total = lax.dynamic_update_slice(
            total, current + jnp.concatenate([added_re, added_im], axis=1), (offset, 0)
        )
        mine = lax.psum_scatter(total, ("col", "dev"), scatter_dimension=0, tiled=True)
        image_re = scale * mine[:, :width]
        image_im = scale * mine[:, width:]
        real_part = real_part + damping * (source + image_re - real_part)
        imag_part = imag_part + damping * (image_im - imag_part)
    return (real_part, imag_part)


def split(value):
    high = value.astype(jnp.bfloat16)
    return high, (value - high.astype(jnp.float32)).astype(jnp.bfloat16)


def dot(left, right):
    return jnp.dot(left, right, preferred_element_type=jnp.float32)


def dot_nt(left, right):
    return lax.dot_general(
        left, right, (((1,), (1,)), ((), ())), preferred_element_type=jnp.float32
    )


def dot3(stacked, rows, right, product=dot):
    high, low = split(right)
    both = product(stacked, high)
    return both[:rows] + both[rows:] + product(stacked[:rows], low)


def stack(value):
    high, low = split(value)
    return jnp.concatenate([high, low], axis=0)


def small(kernel, name, scalars, out_shape, scratch, cost, *operands, chi=None, limit=LIMIT):
    vmem = pl.BlockSpec(memory_space=pltpu.VMEM)
    in_specs = [pl.BlockSpec(memory_space=pltpu.SMEM)] + [vmem] * len(operands)
    if chi is not None:
        in_specs.append(pl.BlockSpec(memory_space=pl.ANY))
        operands += (chi,)
    return pl.pallas_call(
        kernel,
        name=name,
        in_specs=in_specs,
        out_specs=[vmem] * len(out_shape),
        out_shape=out_shape,
        scratch_shapes=scratch,
        cost_estimate=pl.CostEstimate(flops=cost[0], bytes_accessed=cost[1], transcendentals=0),
        compiler_params=pltpu.CompilerParams(vmem_limit_bytes=limit * MIB),
    )(scalars, *operands)


def shaped(*shape):
    return jax.ShapeDtypeStruct(shape, jnp.float32)


def product3(stacked, rows, high, low):
    both = dot(stacked, high)
    return both[:rows] + both[rows:] + dot(stacked[:rows], low)


def fill_panel(panel, core, near, far, width):
    rows, half = near.shape
    for piece, place in ((near, core), (far, 1 - core)):
        at = pl.ds(pl.multiple_of(place * half, half), half)
        high, low = split(piece[...])
        panel[0, :rows, at] = high
        panel[0, rows:, at] = low
        if rows == 2 * width:
            panel[1, :width, at] = -high[width:]
            panel[1, width:rows, at] = high[:width]
            panel[1, rows : rows + width, at] = -low[width:]
            panel[1, rows + width :, at] = low[:width]


def add_product(total, width, panel, part, block, first):
    if panel.shape[0] == 2:
        rows, stacked, at = 2 * width, panel[part], slice(None)
    else:
        rows, stacked, at = width, panel[0], slice(part * width, (part + 1) * width)
    product = product3(stacked, rows, *split(block))
    total[at] = product if first else total[at] + product


def fetch(scalars, chi, targets, sems, jobs):
    slab = targets[0].shape[-1]
    queue = []
    for (j, far), target in zip(jobs, targets):
        pair = 1 - scalars[0] if far else scalars[0]
        at = pl.ds(pl.multiple_of((scalars[2] ^ j) * slab, slab), slab)
        for part in range(2):
            source = chi.at[part, pl.ds(2 * pair, 2), 0, :, at]
            queue.append(pltpu.make_async_copy(source, target.at[part], sems.at[len(queue)]))
    for copy in queue[:DEPTH]:
        copy.start()

    def arrived(index):
        queue[index].wait()
        if index + DEPTH < len(queue):
            queue[index + DEPTH].start()

    return arrived


def begin_kernel(scalars, source, coulomb, bare, scaled):
    turned = source[...].T
    bare[...] = turned
    scaled[...] = turned * coulomb[...][None, :]


def first_kernel(width, jobs, scalars, near, far, chi, out, *rest):
    *blocks, panel, sems = rest
    slab = 2 * near.shape[1]
    arrived = fetch(scalars, chi, blocks, sems, jobs)
    fill_panel(panel, scalars[1], near, far, width)
    for part in range(2):
        arrived(part)
        first = part == 0 or panel.shape[0] == 1
        add_product(out.at[0], width, panel, part, blocks[0][part].reshape(slab, slab), first)
    for index in range(2, 2 * len(jobs)):
        arrived(index)


def near_kernel(width, scalars, near, far, *rest):
    *blocks, out, panel = rest
    slab = 2 * near.shape[1]
    fill_panel(panel, scalars[1], near, far, width)
    for index, block in enumerate(blocks):
        for part in range(2):
            first = part == 0 or panel.shape[0] == 1
            add_product(out.at[index], width, panel, part, block[part].reshape(slab, slab), first)


def halves_out(scalars, full, send, keep):
    half = send.shape[1]
    for place, out in ((1 - scalars[3], send), (scalars[3], keep)):
        out[...] = full[:, pl.ds(pl.multiple_of(place * half, half), half)]


def far_kernel(width, begun, scalars, near, far, start, block, send, keep, panel, full):
    slab = 2 * near.shape[1]
    full[...] = start[begun]
    fill_panel(panel, scalars[1], near, far, width)
    for part in range(2):
        add_product(full, width, panel, part, block[part].reshape(slab, slab), False)
    halves_out(scalars, full, send, keep)


def held_kernel(width, scalars, near, near_far, far, far_far, near_block, far_block, send, keep, panel, full):
    slab = 2 * near.shape[1]
    for side, pieces in enumerate(((near, near_far), (far, far_far))):
        fill_panel(panel.at[side], scalars[1], *pieces, width)
    for side, block in enumerate((near_block, far_block)):
        for part in range(2):
            first = side == 0 and (part == 0 or panel.shape[1] == 1)
            add_product(full, width, panel.at[side], part, block[part].reshape(slab, slab), first)
    halves_out(scalars, full, send, keep)


def both_kernel(width, jobs, scalars, near, near_far, far, far_far, chi, *rest):
    count = len(jobs) // 2
    outs, blocks, (panel, full, sems) = rest[: 2 * count], rest[2 * count : 4 * count], rest[4 * count :]
    slab = 2 * near.shape[1]
    arrived = fetch(scalars, chi, blocks, sems, jobs)
    fill_panel(panel.at[0], scalars[1], near, near_far, width)
    fill_panel(panel.at[1], scalars[1], far, far_far, width)
    for index, block in enumerate(blocks):
        side = index % 2
        for part in range(2):
            arrived(2 * index + part)
            first = side == 0 and (part == 0 or panel.shape[1] == 1)
            add_product(full, width, panel.at[side], part, block[part].reshape(slab, slab), first)
        if side == 1:
            halves_out(scalars, full, outs[index - 1], outs[index])


def project_kernel(width, scalars, near, far, rho_re, rho_im, keep, send, full):
    rows, half = near.shape
    dev, core = scalars[3], scalars[1]
    total_re = total_im = None
    for piece, place in ((near, dev), (far, 1 - dev)):
        at = pl.ds(pl.multiple_of(place * half, half), half)
        panel = stack(piece[...])
        by_re = dot3(panel, rows, rho_re[at])
        by_im = dot3(panel, rows, rho_im[at])
        total_re = by_re if total_re is None else total_re + by_re
        total_im = by_im if total_im is None else total_im + by_im
    if rows == 2 * width:
        full[:width] = total_re[:width] + total_im[width:]
        full[width:] = total_re[width:] - total_im[:width]
    else:
        full[:width] = total_re
        full[width:] = -total_im
    keep[...] = full[pl.ds(pl.multiple_of(core * width, width), width)]
    send[...] = full[pl.ds(pl.multiple_of((1 - core) * width, width), width)]


def spread_kernel(width, scalars, near, far, weight, rho_re, rho_im, first, second, first_out, second_out, full):
    half = first.shape[1]
    dev, core = scalars[3], scalars[1]
    full[pl.ds(pl.multiple_of(core * width, width), width)] = weight[...] * near[...]
    full[pl.ds(pl.multiple_of((1 - core) * width, width), width)] = weight[...] * far[...]
    panel = stack(full[...])
    for place, given, out in ((1 - dev, first, first_out), (dev, second, second_out)):
        at = pl.ds(pl.multiple_of(place * half, half), half)
        by_re = dot3(panel, 2 * width, rho_re[at], dot_nt)
        by_im = dot3(panel, 2 * width, rho_im[at], dot_nt)
        out[:width] = given[:width] - (by_re[:width] - by_im[width:])
        out[width:] = given[width:] - (by_re[width:] + by_im[:width])


def end_kernel(width, scalars, own, by_dev, iterate, bare, coulomb, out_re, out_im):
    image = coulomb[...] * (own[...] + by_dev[...])
    real_part = iterate[:width]
    imag_part = iterate[width:]
    real_part = real_part + damping * (bare[...] + image[:width] - real_part)
    imag_part = imag_part + damping * (image[width:] - imag_part)
    out_re[...] = real_part.T
    out_im[...] = imag_part.T


def after(value, *earlier):
    return lax.optimization_barrier((value, *earlier))[0]


def exchange(value, axis, flip):
    size = lax.axis_size(axis)
    return lax.ppermute(value, axis, [(i, i ^ flip) for i in range(size)])


def exchanged(rho_re, rho_im, coulomb, chi_prev, source, band_v, band_c, band_energy, band_occ):
    weight = pair_weight(band_v, band_c, band_energy, band_occ)[None, :]
    half, width = source.shape
    pairs = rho_re.shape[1]
    slab = 2 * half
    panel_rows = 2 * width
    parts = chi_prev.shape[0]
    row_block = chi_prev.shape[4]
    n_slab = row_block // slab
    last = n_slab - 1
    grp = lax.axis_index("grp")
    scalars = jnp.stack([grp // 2, grp % 2, lax.axis_index("col"), lax.axis_index("dev")]).astype(jnp.int32)
    scale = coulomb[None, :]

    bare, scaled = small(
        begin_kernel, "begin", scalars, [shaped(width, half)] * 2, [], (0, 12 * half * width), source, coulomb
    )

    def products(blocks, rows):
        flops = 3 * 2 * 2 * blocks * rows * slab * slab
        return flops, 4 * blocks * slab * (parts * slab + panel_rows)

    block_shape = (parts, 2, half, slab)

    def image(scaled, blocks):
        rows = scaled.shape[0]
        from_x = exchange(scaled, "grp", 2)
        from_core = exchange(scaled, "grp", 1)
        from_dev = exchange(scaled, "dev", 1)
        panel_shape = (rows // width, 2 * rows, slab)
        panel = pltpu.VMEM(panel_shape, jnp.bfloat16)
        full = pltpu.VMEM((panel_rows, slab), jnp.float32)
        fresh = not blocks


        if fresh:
            jobs = [(last, False), (last, True)]
            start, *brought = small(
                functools.partial(first_kernel, width, jobs), "first_near", scalars,
                [shaped(1, panel_rows, slab)] + [shaped(*block_shape)] * 2,
                [panel, pltpu.SemaphoreType.DMA((4,))], products(1, rows), scaled, from_core, chi=chi_prev,
            )
            blocks.update(zip(jobs, brought))
        else:
            (start,) = small(
                functools.partial(near_kernel, width), "near_half", scalars, [shaped(AHEAD, panel_rows, slab)],
                [panel], products(AHEAD, rows), scaled, from_core, *[blocks[last - i, False] for i in range(AHEAD)],
            )

        from_x = after(from_x, start)
        from_x_core = exchange(from_x, "grp", 1)
        def far_slab(j, *earlier):
            return small(
                functools.partial(far_kernel, width, last - j), f"far_slab_{j}", scalars,
                [shaped(panel_rows, half)] * 2, [panel, full], products(1, rows),
                from_x, after(from_x_core, *earlier), start, blocks[j, True],
            )

        def held_slab(j, *earlier):
            return small(
                functools.partial(held_kernel, width), f"held_slab_{j}", scalars,
                [shaped(panel_rows, half)] * 2, [pltpu.VMEM((2, *panel_shape), jnp.bfloat16), full],
                products(2, rows),
                scaled, from_core, from_x, after(from_x_core, *earlier), blocks[j, False], blocks[j, True],
            )

        def both_slab(j, *earlier):
            jobs = [(j, False), (j, True)]
            *outs, near_block, far_block = small(
                functools.partial(both_kernel, width, jobs), f"both_slabs_{j}", scalars,
                [shaped(panel_rows, half)] * 2 + [shaped(*block_shape)] * 2,
                [pltpu.VMEM((2, *panel_shape), jnp.bfloat16), full, pltpu.SemaphoreType.DMA((4,))],
                products(2, rows), scaled, from_core, from_x, after(from_x_core, *earlier), chi=chi_prev,
            )
            blocks.update(zip(jobs, (near_block, far_block)))
            return outs

        def slab_of(j, *earlier):
            if fresh:
                return both_slab(j, *earlier)
            return (far_slab if last - j < AHEAD else held_slab)(j, *earlier)

        send3, keep3 = far_slab(3, start, from_dev)
        got3 = exchange(send3, "dev", 1)
        keep, send = small(
            functools.partial(project_kernel, width), "project", scalars, [shaped(width, pairs)] * 2,
            [pltpu.VMEM((panel_rows, pairs), jnp.float32)],
            (3 * 4 * rows * slab * pairs, 8 * slab * pairs),
            scaled, after(from_dev, start, send3), rho_re, rho_im,
        )
        total = keep + exchange(send, "grp", 1)
        send2, keep2 = slab_of(2, send3, total)
        got2 = exchange(send2, "dev", 1)
        total = total + exchange(total, "col", 1)
        sum3 = keep3 + after(got3, total)
        across = exchange(sum3, "col", 1)
        send1, keep1 = slab_of(1, send2, total, sum3)
        got1 = exchange(send1, "dev", 1)
        total = total + after(exchange(total, "grp", 2), send1)
        sum2 = keep2 + got2 + across
        far = exchange(sum2, "col", 2)
        send0, keep0 = slab_of(0, send1, total)
        total = total + after(exchange(total, "col", 2), send0)
        other = exchange(total, "grp", 1)
        sum1 = keep1 + after(got1, send0)
        near = exchange(sum1, "col", 1)
        send0, keep0 = small(
            functools.partial(spread_kernel, width), "spread", scalars, [shaped(panel_rows, half)] * 2,
            [pltpu.VMEM((panel_rows, pairs), jnp.float32)],
            (3 * 4 * panel_rows * slab * pairs, 8 * slab * pairs),
            total, after(other, sum1), weight, rho_re, rho_im, send0, keep0,
        )
        got0 = exchange(send0, "dev", 1)
        mine = keep0 + far
        mine = mine + after(near, mine)
        return mine, after(got0, mine)

    blocks = {}
    mine, by_dev = image(scaled, blocks)
    pulled = scale * (mine + by_dev)
    real_part = bare + damping * (bare + pulled[:width] - bare)
    imag_part = damping * pulled[width:]
    iterate = jnp.concatenate([real_part, imag_part], axis=0)
    for sweep in range(1, ITERS):
        mine, by_dev = image(scale * iterate, blocks)
    return small(
        functools.partial(end_kernel, width), "end", scalars, [shaped(half, width)] * 2,
        [], (0, 4 * 8 * half * panel_rows),
        mine, by_dev, iterate, bare, scale,
    )


def solution(mesh):
    placed = (
        P(("grp", "col"), "dev"),
        P(("grp", "col"), "dev"),
        P(("grp", "col", "dev")),
        P(None, None, "col", "dev", "grp"),
        P(("grp", "col", "dev"), None),
        P("dev"),
        P("dev"),
        P(),
        P(),
    )

    def shards(*blocks):
        half, width = blocks[4].shape
        pairs = blocks[0].shape[1]
        paired = mesh.shape["grp"] == 4 and mesh.shape["col"] == 4 and mesh.shape["dev"] == 2
        tiled = half % 128 == 0 and width % 128 == 0 and pairs % 128 == 0
        return (exchanged if paired and tiled and ITERS == 2 else general)(*blocks)

    return jax.shard_map(
        shards,
        mesh=mesh,
        in_specs=placed,
        out_specs=(P(("grp", "col", "dev"), None), P(("grp", "col", "dev"), None)),
        check_vma=False,
    )
```

```python
import functools

import jax
import jax.numpy as jnp
from jax import lax
from jax.experimental import pallas as pl
from jax.experimental.pallas import tpu as pltpu
from jax.sharding import PartitionSpec as P

ITERS = 2


frequency = 0.8
damping = 0.5
MIB = 1 << 20
DEPTH = 4
LIMIT = 8
AHEAD = 3


def lookup(bands, table):
    band_index = jnp.arange(table.shape[0], dtype=jnp.int32)
    match = bands[None, :] == band_index[:, None]
    return jnp.sum(jnp.where(match, table[:, None], 0.0), axis=0)


def pair_weight(band_v, band_c, band_energy, band_occ):
    delta = lookup(band_c, band_energy) - lookup(band_v, band_energy)
    filling = lookup(band_v, band_occ) - lookup(band_c, band_occ)
    return filling * 2.0 * delta / (delta * delta + frequency * frequency)


def contract(left, right):
    return lax.dot_general(
        left,
        right,
        (((0,), (0,)), ((), ())),
        precision=lax.Precision.HIGHEST,
        preferred_element_type=jnp.float32,
    )


def matmul(left, right):
    return jnp.dot(left, right, precision=lax.Precision.HIGHEST, preferred_element_type=jnp.float32)


def general(rho_re, rho_im, coulomb, chi_prev, source, band_v, band_c, band_energy, band_occ):
    weight = pair_weight(band_v, band_c, band_energy, band_occ)
    slab = rho_re.shape[0]
    width = source.shape[1]
    row_block = chi_prev.shape[4]
    my_cols = chi_prev.shape[1] * chi_prev.shape[3]
    previous = chi_prev.reshape(2, my_cols, row_block)
    scale = coulomb[:, None]
    real_part = source
    imag_part = jnp.zeros_like(source)
    for sweep in range(ITERS):
        scaled = jnp.concatenate([scale * real_part, scale * imag_part], axis=1)
        piece = lax.all_gather(scaled, "grp", axis=0, tiled=True)
        swapped = jnp.concatenate([-piece[:, width:], piece[:, :width]], axis=1)
        total = contract(previous[0], piece) + contract(previous[1], swapped)
        slab_scaled = lax.all_gather(scaled, "dev", axis=0, tiled=True)
        slab_re = slab_scaled[:, :width]
        slab_im = slab_scaled[:, width:]
        proj_re = contract(rho_re, slab_re) + contract(rho_im, slab_im)
        proj_im = contract(rho_re, slab_im) - contract(rho_im, slab_re)
        summed = lax.psum(jnp.concatenate([proj_re, proj_im], axis=1), ("grp", "col"))
        weighted = weight[:, None] * summed
        weighted_re = weighted[:, :width]
        weighted_im = weighted[:, width:]
        added_re = -(matmul(rho_re, weighted_re) - matmul(rho_im, weighted_im))
        added_im = -(matmul(rho_re, weighted_im) + matmul(rho_im, weighted_re))
        offset = lax.axis_index("col") * slab
        current = lax.dynamic_slice(total, (offset, 0), (slab, 2 * width))
        total = lax.dynamic_update_slice(
            total, current + jnp.concatenate([added_re, added_im], axis=1), (offset, 0)
        )
        mine = lax.psum_scatter(total, ("col", "dev"), scatter_dimension=0, tiled=True)
        image_re = scale * mine[:, :width]
        image_im = scale * mine[:, width:]
        real_part = real_part + damping * (source + image_re - real_part)
        imag_part = imag_part + damping * (image_im - imag_part)
    return (real_part, imag_part)


def split(value):
    high = value.astype(jnp.bfloat16)
    return high, (value - high.astype(jnp.float32)).astype(jnp.bfloat16)


def dot(left, right):
    return jnp.dot(left, right, preferred_element_type=jnp.float32)


def dot_nt(left, right):
    return lax.dot_general(
        left, right, (((1,), (1,)), ((), ())), preferred_element_type=jnp.float32
    )


def dot3(stacked, rows, right, product=dot):
    high, low = split(right)
    both = product(stacked, high)
    return both[:rows] + both[rows:] + product(stacked[:rows], low)


def stack(value):
    high, low = split(value)
    return jnp.concatenate([high, low], axis=0)


def small(kernel, name, scalars, out_shape, scratch, cost, *operands, chi=None, limit=LIMIT):
    vmem = pl.BlockSpec(memory_space=pltpu.VMEM)
    in_specs = [pl.BlockSpec(memory_space=pltpu.SMEM)] + [vmem] * len(operands)
    if chi is not None:
        in_specs.append(pl.BlockSpec(memory_space=pl.ANY))
        operands += (chi,)
    return pl.pallas_call(
        kernel,
        name=name,
        in_specs=in_specs,
        out_specs=[vmem] * len(out_shape),
        out_shape=out_shape,
        scratch_shapes=scratch,
        cost_estimate=pl.CostEstimate(flops=cost[0], bytes_accessed=cost[1], transcendentals=0),
        compiler_params=pltpu.CompilerParams(vmem_limit_bytes=limit * MIB),
    )(scalars, *operands)


def shaped(*shape):
    return jax.ShapeDtypeStruct(shape, jnp.float32)


def product3(stacked, rows, high, low):
    both = dot(stacked, high)
    return both[:rows] + both[rows:] + dot(stacked[:rows], low)


def fill_panel(panel, core, near, far, width):
    rows, half = near.shape
    for piece, place in ((near, core), (far, 1 - core)):
        at = pl.ds(pl.multiple_of(place * half, half), half)
        high, low = split(piece[...])
        panel[0, :rows, at] = high
        panel[0, rows:, at] = low
        if rows == 2 * width:
            panel[1, :width, at] = -high[width:]
            panel[1, width:rows, at] = high[:width]
            panel[1, rows : rows + width, at] = -low[width:]
            panel[1, rows + width :, at] = low[:width]


def add_product(total, width, panel, part, block, first):
    if panel.shape[0] == 2:
        rows, stacked, at = 2 * width, panel[part], slice(None)
    else:
        rows, stacked, at = width, panel[0], slice(part * width, (part + 1) * width)
    product = product3(stacked, rows, *split(block))
    total[at] = product if first else total[at] + product


def fetch(scalars, chi, targets, sems, jobs):
    slab = targets[0].shape[-1]
    queue = []
    for (j, far), target in zip(jobs, targets):
        pair = 1 - scalars[0] if far else scalars[0]
        at = pl.ds(pl.multiple_of((scalars[2] ^ j) * slab, slab), slab)
        for part in range(2):
            source = chi.at[part, pl.ds(2 * pair, 2), 0, :, at]
            queue.append(pltpu.make_async_copy(source, target.at[part], sems.at[len(queue)]))
    for copy in queue[:DEPTH]:
        copy.start()

    def arrived(index):
        queue[index].wait()
        if index + DEPTH < len(queue):
            queue[index + DEPTH].start()

    return arrived


def begin_kernel(source, coulomb, bare, scaled, source_here, coulomb_here, sems):
    copies = [
        pltpu.make_async_copy(source, source_here, sems.at[0]),
        pltpu.make_async_copy(coulomb, coulomb_here, sems.at[1]),
    ]
    for copy in copies:
        copy.start()
    for copy in copies:
        copy.wait()
    turned = source_here[...].T
    bare[...] = turned
    scaled[...] = turned * coulomb_here[...][None, :]


def first_kernel(width, jobs, scalars, near, far, chi, out, *rest):
    *blocks, panel, sems = rest
    slab = 2 * near.shape[1]
    arrived = fetch(scalars, chi, blocks, sems, jobs)
    fill_panel(panel, scalars[1], near, far, width)
    for part in range(2):
        arrived(part)
        first = part == 0 or panel.shape[0] == 1
        add_product(out.at[0], width, panel, part, blocks[0][part].reshape(slab, slab), first)
    for index in range(2, 2 * len(jobs)):
        arrived(index)


def near_kernel(width, scalars, near, far, *rest):
    *blocks, out, panel = rest
    slab = 2 * near.shape[1]
    fill_panel(panel, scalars[1], near, far, width)
    for index, block in enumerate(blocks):
        for part in range(2):
            first = part == 0 or panel.shape[0] == 1
            add_product(out.at[index], width, panel, part, block[part].reshape(slab, slab), first)


def halves_out(scalars, full, send, keep):
    half = send.shape[1]
    for place, out in ((1 - scalars[3], send), (scalars[3], keep)):
        out[...] = full[:, pl.ds(pl.multiple_of(place * half, half), half)]


def far_kernel(width, begun, scalars, near, far, start, block, send, keep, panel, full):
    slab = 2 * near.shape[1]
    full[...] = start[begun]
    fill_panel(panel, scalars[1], near, far, width)
    for part in range(2):
        add_product(full, width, panel, part, block[part].reshape(slab, slab), False)
    halves_out(scalars, full, send, keep)


def held_kernel(width, scalars, near, near_far, far, far_far, near_block, far_block, send, keep, panel, full):
    slab = 2 * near.shape[1]
    for side, pieces in enumerate(((near, near_far), (far, far_far))):
        fill_panel(panel.at[side], scalars[1], *pieces, width)
    for side, block in enumerate((near_block, far_block)):
        for part in range(2):
            first = side == 0 and (part == 0 or panel.shape[1] == 1)
            add_product(full, width, panel.at[side], part, block[part].reshape(slab, slab), first)
    halves_out(scalars, full, send, keep)


def both_kernel(width, jobs, scalars, near, near_far, far, far_far, chi, *rest):
    count = len(jobs) // 2
    outs, blocks, (panel, full, sems) = rest[: 2 * count], rest[2 * count : 4 * count], rest[4 * count :]
    slab = 2 * near.shape[1]
    arrived = fetch(scalars, chi, blocks, sems, jobs)
    fill_panel(panel.at[0], scalars[1], near, near_far, width)
    fill_panel(panel.at[1], scalars[1], far, far_far, width)
    for index, block in enumerate(blocks):
        side = index % 2
        for part in range(2):
            arrived(2 * index + part)
            first = side == 0 and (part == 0 or panel.shape[1] == 1)
            add_product(full, width, panel.at[side], part, block[part].reshape(slab, slab), first)
        if side == 1:
            halves_out(scalars, full, outs[index - 1], outs[index])


def project_kernel(width, scalars, near, far, rho_re, rho_im, keep, send, full):
    rows, half = near.shape
    dev, core = scalars[3], scalars[1]
    total_re = total_im = None
    for piece, place in ((near, dev), (far, 1 - dev)):
        at = pl.ds(pl.multiple_of(place * half, half), half)
        panel = stack(piece[...])
        by_re = dot3(panel, rows, rho_re[at])
        by_im = dot3(panel, rows, rho_im[at])
        total_re = by_re if total_re is None else total_re + by_re
        total_im = by_im if total_im is None else total_im + by_im
    if rows == 2 * width:
        full[:width] = total_re[:width] + total_im[width:]
        full[width:] = total_re[width:] - total_im[:width]
    else:
        full[:width] = total_re
        full[width:] = -total_im
    keep[...] = full[pl.ds(pl.multiple_of(core * width, width), width)]
    send[...] = full[pl.ds(pl.multiple_of((1 - core) * width, width), width)]


def spread_kernel(width, scalars, near, far, weight, rho_re, rho_im, first, second, first_out, second_out, full):
    half = first.shape[1]
    dev, core = scalars[3], scalars[1]
    full[pl.ds(pl.multiple_of(core * width, width), width)] = weight[...] * near[...]
    full[pl.ds(pl.multiple_of((1 - core) * width, width), width)] = weight[...] * far[...]
    panel = stack(full[...])
    for place, given, out in ((1 - dev, first, first_out), (dev, second, second_out)):
        at = pl.ds(pl.multiple_of(place * half, half), half)
        by_re = dot3(panel, 2 * width, rho_re[at], dot_nt)
        by_im = dot3(panel, 2 * width, rho_im[at], dot_nt)
        out[:width] = given[:width] - (by_re[:width] - by_im[width:])
        out[width:] = given[width:] - (by_re[width:] + by_im[:width])


def end_kernel(width, scalars, own, by_dev, iterate, bare, coulomb, out_re, out_im):
    image = coulomb[...] * (own[...] + by_dev[...])
    real_part = iterate[:width]
    imag_part = iterate[width:]
    real_part = real_part + damping * (bare[...] + image[:width] - real_part)
    imag_part = imag_part + damping * (image[width:] - imag_part)
    out_re[...] = real_part.T
    out_im[...] = imag_part.T


def after(value, *earlier):
    return lax.optimization_barrier((value, *earlier))[0]


def exchange(value, axis, flip):
    size = lax.axis_size(axis)
    return lax.ppermute(value, axis, [(i, i ^ flip) for i in range(size)])


def exchanged(rho_re, rho_im, coulomb, chi_prev, source, band_v, band_c, band_energy, band_occ):
    weight = pair_weight(band_v, band_c, band_energy, band_occ)[None, :]
    half, width = source.shape
    pairs = rho_re.shape[1]
    slab = 2 * half
    panel_rows = 2 * width
    parts = chi_prev.shape[0]
    row_block = chi_prev.shape[4]
    n_slab = row_block // slab
    last = n_slab - 1
    grp = lax.axis_index("grp")
    scalars = jnp.stack([grp // 2, grp % 2, lax.axis_index("col"), lax.axis_index("dev")]).astype(jnp.int32)
    scale = coulomb[None, :]

    bare, scaled = pl.pallas_call(
        begin_kernel,
        name="begin",
        in_specs=[pl.BlockSpec(memory_space=pl.ANY)] * 2,
        out_specs=[pl.BlockSpec(memory_space=pltpu.VMEM)] * 2,
        out_shape=[shaped(width, half)] * 2,
        scratch_shapes=[
            pltpu.VMEM((half, width), jnp.float32),
            pltpu.VMEM((half,), jnp.float32),
            pltpu.SemaphoreType.DMA((2,)),
        ],
        cost_estimate=pl.CostEstimate(flops=0, bytes_accessed=12 * half * width, transcendentals=0),
        compiler_params=pltpu.CompilerParams(vmem_limit_bytes=LIMIT * MIB),
    )(source, coulomb)

    def products(blocks, rows):
        flops = 3 * 2 * 2 * blocks * rows * slab * slab
        return flops, 4 * blocks * slab * (parts * slab + panel_rows)

    block_shape = (parts, 2, half, slab)

    def image(scaled, blocks):
        rows = scaled.shape[0]
        from_x = exchange(scaled, "grp", 2)
        from_core = exchange(scaled, "grp", 1)
        from_dev = exchange(scaled, "dev", 1)
        panel_shape = (rows // width, 2 * rows, slab)
        panel = pltpu.VMEM(panel_shape, jnp.bfloat16)
        full = pltpu.VMEM((panel_rows, slab), jnp.float32)
        fresh = not blocks


        if fresh:
            jobs = [(last, False), (last, True)]
            start, *brought = small(
                functools.partial(first_kernel, width, jobs), "first_near", scalars,
                [shaped(1, panel_rows, slab)] + [shaped(*block_shape)] * 2,
                [panel, pltpu.SemaphoreType.DMA((4,))], products(1, rows), scaled, from_core, chi=chi_prev,
            )
            blocks.update(zip(jobs, brought))
        else:
            (start,) = small(
                functools.partial(near_kernel, width), "near_half", scalars, [shaped(AHEAD, panel_rows, slab)],
                [panel], products(AHEAD, rows), scaled, from_core, *[blocks[last - i, False] for i in range(AHEAD)],
            )

        from_x = after(from_x, start)
        from_x_core = exchange(from_x, "grp", 1)
        def far_slab(j, *earlier):
            return small(
                functools.partial(far_kernel, width, last - j), f"far_slab_{j}", scalars,
                [shaped(panel_rows, half)] * 2, [panel, full], products(1, rows),
                from_x, after(from_x_core, *earlier), start, blocks[j, True],
            )

        def held_slab(j, *earlier):
            return small(
                functools.partial(held_kernel, width), f"held_slab_{j}", scalars,
                [shaped(panel_rows, half)] * 2, [pltpu.VMEM((2, *panel_shape), jnp.bfloat16), full],
                products(2, rows),
                scaled, from_core, from_x, after(from_x_core, *earlier), blocks[j, False], blocks[j, True],
            )

        def both_slab(j, *earlier):
            jobs = [(j, False), (j, True)]
            *outs, near_block, far_block = small(
                functools.partial(both_kernel, width, jobs), f"both_slabs_{j}", scalars,
                [shaped(panel_rows, half)] * 2 + [shaped(*block_shape)] * 2,
                [pltpu.VMEM((2, *panel_shape), jnp.bfloat16), full, pltpu.SemaphoreType.DMA((4,))],
                products(2, rows), scaled, from_core, from_x, after(from_x_core, *earlier), chi=chi_prev,
            )
            blocks.update(zip(jobs, (near_block, far_block)))
            return outs

        def slab_of(j, *earlier):
            if fresh:
                return both_slab(j, *earlier)
            return (far_slab if last - j < AHEAD else held_slab)(j, *earlier)

        send3, keep3 = far_slab(3, start, from_dev)
        got3 = exchange(send3, "dev", 1)
        keep, send = small(
            functools.partial(project_kernel, width), "project", scalars, [shaped(width, pairs)] * 2,
            [pltpu.VMEM((panel_rows, pairs), jnp.float32)],
            (3 * 4 * rows * slab * pairs, 8 * slab * pairs),
            scaled, after(from_dev, start, send3), rho_re, rho_im,
        )
        total = keep + exchange(send, "grp", 1)
        send2, keep2 = slab_of(2, send3, total)
        got2 = exchange(send2, "dev", 1)
        total = total + exchange(total, "col", 1)
        sum3 = keep3 + after(got3, total)
        across = exchange(sum3, "col", 1)
        send1, keep1 = slab_of(1, send2, total, sum3)
        got1 = exchange(send1, "dev", 1)
        total = total + after(exchange(total, "grp", 2), send1)
        sum2 = keep2 + got2 + across
        far = exchange(sum2, "col", 2)
        send0, keep0 = slab_of(0, send1, total)
        total = total + after(exchange(total, "col", 2), send0)
        other = exchange(total, "grp", 1)
        sum1 = keep1 + after(got1, send0)
        near = exchange(sum1, "col", 1)
        send0, keep0 = small(
            functools.partial(spread_kernel, width), "spread", scalars, [shaped(panel_rows, half)] * 2,
            [pltpu.VMEM((panel_rows, pairs), jnp.float32)],
            (3 * 4 * panel_rows * slab * pairs, 8 * slab * pairs),
            total, after(other, sum1), weight, rho_re, rho_im, send0, keep0,
        )
        got0 = exchange(send0, "dev", 1)
        mine = keep0 + far
        mine = mine + after(near, mine)
        return mine, after(got0, mine)

    blocks = {}
    mine, by_dev = image(scaled, blocks)
    pulled = scale * (mine + by_dev)
    real_part = bare + damping * (bare + pulled[:width] - bare)
    imag_part = damping * pulled[width:]
    iterate = jnp.concatenate([real_part, imag_part], axis=0)
    for sweep in range(1, ITERS):
        mine, by_dev = image(scale * iterate, blocks)
    return small(
        functools.partial(end_kernel, width), "end", scalars, [shaped(half, width)] * 2,
        [], (0, 4 * 8 * half * panel_rows),
        mine, by_dev, iterate, bare, scale,
    )


def solution(mesh):
    placed = (
        P(("grp", "col"), "dev"),
        P(("grp", "col"), "dev"),
        P(("grp", "col", "dev")),
        P(None, None, "col", "dev", "grp"),
        P(("grp", "col", "dev"), None),
        P("dev"),
        P("dev"),
        P(),
        P(),
    )

    def shards(*blocks):
        half, width = blocks[4].shape
        pairs = blocks[0].shape[1]
        paired = mesh.shape["grp"] == 4 and mesh.shape["col"] == 4 and mesh.shape["dev"] == 2
        tiled = half % 128 == 0 and width % 128 == 0 and pairs % 128 == 0
        return (exchanged if paired and tiled and ITERS == 2 else general)(*blocks)

    return jax.shard_map(
        shards,
        mesh=mesh,
        in_specs=placed,
        out_specs=(P(("grp", "col", "dev"), None), P(("grp", "col", "dev"), None)),
        check_vma=False,
    )
```

```python
import functools

import jax
import jax.numpy as jnp
from jax import lax
from jax.experimental import pallas as pl
from jax.experimental.pallas import tpu as pltpu
from jax.sharding import PartitionSpec as P

ITERS = 2


frequency = 0.8
damping = 0.5
MIB = 1 << 20
DEPTH = 4
LIMIT = 8
AHEAD = 3


def lookup(bands, table):
    band_index = jnp.arange(table.shape[0], dtype=jnp.int32)
    match = bands[None, :] == band_index[:, None]
    return jnp.sum(jnp.where(match, table[:, None], 0.0), axis=0)


def pair_weight(band_v, band_c, band_energy, band_occ):
    delta = lookup(band_c, band_energy) - lookup(band_v, band_energy)
    filling = lookup(band_v, band_occ) - lookup(band_c, band_occ)
    return filling * 2.0 * delta / (delta * delta + frequency * frequency)


def contract(left, right):
    return lax.dot_general(
        left,
        right,
        (((0,), (0,)), ((), ())),
        precision=lax.Precision.HIGHEST,
        preferred_element_type=jnp.float32,
    )


def matmul(left, right):
    return jnp.dot(left, right, precision=lax.Precision.HIGHEST, preferred_element_type=jnp.float32)


def general(rho_re, rho_im, coulomb, chi_prev, source, band_v, band_c, band_energy, band_occ):
    weight = pair_weight(band_v, band_c, band_energy, band_occ)
    slab = rho_re.shape[0]
    width = source.shape[1]
    row_block = chi_prev.shape[4]
    my_cols = chi_prev.shape[1] * chi_prev.shape[3]
    previous = chi_prev.reshape(2, my_cols, row_block)
    scale = coulomb[:, None]
    real_part = source
    imag_part = jnp.zeros_like(source)
    for sweep in range(ITERS):
        scaled = jnp.concatenate([scale * real_part, scale * imag_part], axis=1)
        piece = lax.all_gather(scaled, "grp", axis=0, tiled=True)
        swapped = jnp.concatenate([-piece[:, width:], piece[:, :width]], axis=1)
        total = contract(previous[0], piece) + contract(previous[1], swapped)
        slab_scaled = lax.all_gather(scaled, "dev", axis=0, tiled=True)
        slab_re = slab_scaled[:, :width]
        slab_im = slab_scaled[:, width:]
        proj_re = contract(rho_re, slab_re) + contract(rho_im, slab_im)
        proj_im = contract(rho_re, slab_im) - contract(rho_im, slab_re)
        summed = lax.psum(jnp.concatenate([proj_re, proj_im], axis=1), ("grp", "col"))
        weighted = weight[:, None] * summed
        weighted_re = weighted[:, :width]
        weighted_im = weighted[:, width:]
        added_re = -(matmul(rho_re, weighted_re) - matmul(rho_im, weighted_im))
        added_im = -(matmul(rho_re, weighted_im) + matmul(rho_im, weighted_re))
        offset = lax.axis_index("col") * slab
        current = lax.dynamic_slice(total, (offset, 0), (slab, 2 * width))
        total = lax.dynamic_update_slice(
            total, current + jnp.concatenate([added_re, added_im], axis=1), (offset, 0)
        )
        mine = lax.psum_scatter(total, ("col", "dev"), scatter_dimension=0, tiled=True)
        image_re = scale * mine[:, :width]
        image_im = scale * mine[:, width:]
        real_part = real_part + damping * (source + image_re - real_part)
        imag_part = imag_part + damping * (image_im - imag_part)
    return (real_part, imag_part)


def split(value):
    high = value.astype(jnp.bfloat16)
    return high, (value - high.astype(jnp.float32)).astype(jnp.bfloat16)


def dot(left, right):
    return jnp.dot(left, right, preferred_element_type=jnp.float32)


def dot_nt(left, right):
    return lax.dot_general(
        left, right, (((1,), (1,)), ((), ())), preferred_element_type=jnp.float32
    )


def dot3(stacked, rows, right, product=dot):
    high, low = split(right)
    both = product(stacked, high)
    return both[:rows] + both[rows:] + product(stacked[:rows], low)


def stack(value):
    high, low = split(value)
    return jnp.concatenate([high, low], axis=0)


def small(kernel, name, scalars, out_shape, scratch, cost, *operands, chi=None, limit=LIMIT):
    vmem = pl.BlockSpec(memory_space=pltpu.VMEM)
    in_specs = [pl.BlockSpec(memory_space=pltpu.SMEM)] + [vmem] * len(operands)
    if chi is not None:
        in_specs.append(pl.BlockSpec(memory_space=pl.ANY))
        operands += (chi,)
    return pl.pallas_call(
        kernel,
        name=name,
        in_specs=in_specs,
        out_specs=[vmem] * len(out_shape),
        out_shape=out_shape,
        scratch_shapes=scratch,
        cost_estimate=pl.CostEstimate(flops=cost[0], bytes_accessed=cost[1], transcendentals=0),
        compiler_params=pltpu.CompilerParams(vmem_limit_bytes=limit * MIB),
    )(scalars, *operands)


def shaped(*shape):
    return jax.ShapeDtypeStruct(shape, jnp.float32)


def product3(stacked, rows, high, low):
    both = dot(stacked, high)
    return both[:rows] + both[rows:] + dot(stacked[:rows], low)


def fill_panel(panel, core, near, far, width):
    rows, half = near.shape
    for piece, place in ((near, core), (far, 1 - core)):
        at = pl.ds(pl.multiple_of(place * half, half), half)
        high, low = split(piece[...])
        panel[0, :rows, at] = high
        panel[0, rows:, at] = low
        if rows == 2 * width:
            panel[1, :width, at] = -high[width:]
            panel[1, width:rows, at] = high[:width]
            panel[1, rows : rows + width, at] = -low[width:]
            panel[1, rows + width :, at] = low[:width]


def add_product(total, width, panel, part, block, first):
    if panel.shape[0] == 2:
        rows, stacked, at = 2 * width, panel[part], slice(None)
    else:
        rows, stacked, at = width, panel[0], slice(part * width, (part + 1) * width)
    product = product3(stacked, rows, *split(block))
    total[at] = product if first else total[at] + product


def fetch(scalars, chi, targets, sems, jobs):
    slab = targets[0].shape[-1]
    queue = []
    for (j, far), target in zip(jobs, targets):
        pair = 1 - scalars[0] if far else scalars[0]
        at = pl.ds(pl.multiple_of((scalars[2] ^ j) * slab, slab), slab)
        for part in range(2):
            source = chi.at[part, pl.ds(2 * pair, 2), 0, :, at]
            queue.append(pltpu.make_async_copy(source, target.at[part], sems.at[len(queue)]))
    for copy in queue[:DEPTH]:
        copy.start()

    def arrived(index):
        queue[index].wait()
        if index + DEPTH < len(queue):
            queue[index + DEPTH].start()

    return arrived


def begin_kernel(source, coulomb, bare, scaled, source_here, coulomb_here, sems):
    copies = [
        pltpu.make_async_copy(source, source_here, sems.at[0]),
        pltpu.make_async_copy(coulomb, coulomb_here, sems.at[1]),
    ]
    for copy in copies:
        copy.start()
    for copy in copies:
        copy.wait()
    turned = source_here[...].T
    bare[...] = turned
    scaled[...] = turned * coulomb_here[...][None, :]


def first_kernel(width, jobs, scalars, near, far, chi, out, *rest):
    *blocks, panel, sems = rest
    slab = 2 * near.shape[1]
    arrived = fetch(scalars, chi, blocks, sems, jobs)
    fill_panel(panel, scalars[1], near, far, width)
    for part in range(2):
        arrived(part)
        first = part == 0 or panel.shape[0] == 1
        add_product(out.at[0], width, panel, part, blocks[0][part].reshape(slab, slab), first)
    for index in range(2, 2 * len(jobs)):
        arrived(index)


def near_kernel(width, scalars, near, far, *rest):
    *blocks, out, panel = rest
    slab = 2 * near.shape[1]
    fill_panel(panel, scalars[1], near, far, width)
    for index, block in enumerate(blocks):
        for part in range(2):
            first = part == 0 or panel.shape[0] == 1
            add_product(out.at[index], width, panel, part, block[part].reshape(slab, slab), first)


def halves_out(scalars, full, send, keep):
    half = send.shape[1]
    for place, out in ((1 - scalars[3], send), (scalars[3], keep)):
        out[...] = full[:, pl.ds(pl.multiple_of(place * half, half), half)]


def far_kernel(width, begun, scalars, near, far, start, block, send, keep, panel, full):
    slab = 2 * near.shape[1]
    full[...] = start[begun]
    fill_panel(panel, scalars[1], near, far, width)
    for part in range(2):
        add_product(full, width, panel, part, block[part].reshape(slab, slab), False)
    halves_out(scalars, full, send, keep)


def held_kernel(width, scalars, near, near_far, far, far_far, near_block, far_block, send, keep, panel, full):
    slab = 2 * near.shape[1]
    for side, pieces in enumerate(((near, near_far), (far, far_far))):
        fill_panel(panel.at[side], scalars[1], *pieces, width)
    for side, block in enumerate((near_block, far_block)):
        for part in range(2):
            first = side == 0 and (part == 0 or panel.shape[1] == 1)
            add_product(full, width, panel.at[side], part, block[part].reshape(slab, slab), first)
    halves_out(scalars, full, send, keep)


def both_kernel(width, jobs, scalars, near, near_far, far, far_far, chi, *rest):
    count = len(jobs) // 2
    outs, blocks, (panel, full, sems) = rest[: 2 * count], rest[2 * count : 4 * count], rest[4 * count :]
    slab = 2 * near.shape[1]
    arrived = fetch(scalars, chi, blocks, sems, jobs)
    fill_panel(panel.at[0], scalars[1], near, near_far, width)
    fill_panel(panel.at[1], scalars[1], far, far_far, width)
    for index, block in enumerate(blocks):
        side = index % 2
        for part in range(2):
            arrived(2 * index + part)
            first = side == 0 and (part == 0 or panel.shape[1] == 1)
            add_product(full, width, panel.at[side], part, block[part].reshape(slab, slab), first)
        if side == 1:
            halves_out(scalars, full, outs[index - 1], outs[index])


def project_kernel(width, scalars, near, far, rho_re, rho_im, keep, send, full):
    rows, half = near.shape
    dev, core = scalars[3], scalars[1]
    total_re = total_im = None
    for piece, place in ((near, dev), (far, 1 - dev)):
        at = pl.ds(pl.multiple_of(place * half, half), half)
        panel = stack(piece[...])
        by_re = dot3(panel, rows, rho_re[at])
        by_im = dot3(panel, rows, rho_im[at])
        total_re = by_re if total_re is None else total_re + by_re
        total_im = by_im if total_im is None else total_im + by_im
    if rows == 2 * width:
        full[:width] = total_re[:width] + total_im[width:]
        full[width:] = total_re[width:] - total_im[:width]
    else:
        full[:width] = total_re
        full[width:] = -total_im
    keep[...] = full[pl.ds(pl.multiple_of(core * width, width), width)]
    send[...] = full[pl.ds(pl.multiple_of((1 - core) * width, width), width)]


def spread_kernel(width, scalars, near, far, weight, rho_re, rho_im, first, second, first_out, second_out, full):
    half = first.shape[1]
    dev, core = scalars[3], scalars[1]
    full[pl.ds(pl.multiple_of(core * width, width), width)] = weight[...] * near[...]
    full[pl.ds(pl.multiple_of((1 - core) * width, width), width)] = weight[...] * far[...]
    panel = stack(full[...])
    for place, given, out in ((1 - dev, first, first_out), (dev, second, second_out)):
        at = pl.ds(pl.multiple_of(place * half, half), half)
        by_re = dot3(panel, 2 * width, rho_re[at], dot_nt)
        by_im = dot3(panel, 2 * width, rho_im[at], dot_nt)
        out[:width] = given[:width] - (by_re[:width] - by_im[width:])
        out[width:] = given[width:] - (by_re[width:] + by_im[:width])


def end_kernel(width, scalars, own, by_dev, iterate, bare, coulomb, out_re, out_im):
    image = coulomb[...] * (own[...] + by_dev[...])
    real_part = iterate[:width]
    imag_part = iterate[width:]
    real_part = real_part + damping * (bare[...] + image[:width] - real_part)
    imag_part = imag_part + damping * (image[width:] - imag_part)
    out_re[...] = real_part.T
    out_im[...] = imag_part.T


def after(value, *earlier):
    return lax.optimization_barrier((value, *earlier))[0]


def exchange(value, axis, flip):
    size = lax.axis_size(axis)
    return lax.ppermute(value, axis, [(i, i ^ flip) for i in range(size)])


def exchanged(rho_re, rho_im, coulomb, chi_prev, source, band_v, band_c, band_energy, band_occ):
    weight = pair_weight(band_v, band_c, band_energy, band_occ)[None, :]
    half, width = source.shape
    pairs = rho_re.shape[1]
    slab = 2 * half
    panel_rows = 2 * width
    parts = chi_prev.shape[0]
    row_block = chi_prev.shape[4]
    n_slab = row_block // slab
    last = n_slab - 1
    grp = lax.axis_index("grp")
    scalars = jnp.stack([grp // 2, grp % 2, lax.axis_index("col"), lax.axis_index("dev")]).astype(jnp.int32)
    scale = coulomb[None, :]

    bare, scaled = pl.pallas_call(
        begin_kernel,
        name="begin",
        in_specs=[pl.BlockSpec(memory_space=pl.ANY)] * 2,
        out_specs=[pl.BlockSpec(memory_space=pltpu.VMEM)] * 2,
        out_shape=[shaped(width, half)] * 2,
        scratch_shapes=[
            pltpu.VMEM((half, width), jnp.float32),
            pltpu.VMEM((half,), jnp.float32),
            pltpu.SemaphoreType.DMA((2,)),
        ],
        cost_estimate=pl.CostEstimate(flops=0, bytes_accessed=12 * half * width, transcendentals=0),
        compiler_params=pltpu.CompilerParams(vmem_limit_bytes=LIMIT * MIB),
    )(source, coulomb)

    def products(blocks, rows):
        flops = 3 * 2 * 2 * blocks * rows * slab * slab
        return flops, 4 * blocks * slab * (parts * slab + panel_rows)

    block_shape = (parts, 2, half, slab)

    def image(scaled, blocks):
        rows = scaled.shape[0]
        from_x = exchange(scaled, "grp", 2)
        from_core = exchange(scaled, "grp", 1)
        from_dev = exchange(scaled, "dev", 1)
        panel_shape = (rows // width, 2 * rows, slab)
        panel = pltpu.VMEM(panel_shape, jnp.bfloat16)
        full = pltpu.VMEM((panel_rows, slab), jnp.float32)
        fresh = not blocks


        if fresh:
            jobs = [(last, False), (last, True)]
            start, *brought = small(
                functools.partial(first_kernel, width, jobs), "first_near", scalars,
                [shaped(1, panel_rows, slab)] + [shaped(*block_shape)] * 2,
                [panel, pltpu.SemaphoreType.DMA((4,))], products(1, rows), scaled, from_core, chi=chi_prev,
            )
            blocks.update(zip(jobs, brought))
        else:
            (start,) = small(
                functools.partial(near_kernel, width), "near_half", scalars, [shaped(AHEAD, panel_rows, slab)],
                [panel], products(AHEAD, rows), scaled, from_core, *[blocks[last - i, False] for i in range(AHEAD)],
            )

        from_x = after(from_x, start)
        from_x_core = exchange(from_x, "grp", 1)
        def far_slab(j, *earlier):
            return small(
                functools.partial(far_kernel, width, last - j), f"far_slab_{j}", scalars,
                [shaped(panel_rows, half)] * 2, [panel, full], products(1, rows),
                from_x, after(from_x_core, *earlier), start, blocks[j, True],
            )

        def held_slab(j, *earlier):
            return small(
                functools.partial(held_kernel, width), f"held_slab_{j}", scalars,
                [shaped(panel_rows, half)] * 2, [pltpu.VMEM((2, *panel_shape), jnp.bfloat16), full],
                products(2, rows),
                scaled, from_core, from_x, after(from_x_core, *earlier), blocks[j, False], blocks[j, True],
            )

        def both_slab(j, *earlier):
            jobs = [(j, False), (j, True)]
            *outs, near_block, far_block = small(
                functools.partial(both_kernel, width, jobs), f"both_slabs_{j}", scalars,
                [shaped(panel_rows, half)] * 2 + [shaped(*block_shape)] * 2,
                [pltpu.VMEM((2, *panel_shape), jnp.bfloat16), full, pltpu.SemaphoreType.DMA((4,))],
                products(2, rows), scaled, from_core, from_x, after(from_x_core, *earlier), chi=chi_prev,
            )
            blocks.update(zip(jobs, (near_block, far_block)))
            return outs

        def slab_of(j, *earlier):
            if fresh:
                return both_slab(j, *earlier)
            return (far_slab if last - j < AHEAD else held_slab)(j, *earlier)

        def project(*earlier):
            return small(
                functools.partial(project_kernel, width), "project", scalars, [shaped(width, pairs)] * 2,
                [pltpu.VMEM((panel_rows, pairs), jnp.float32)],
                (3 * 4 * rows * slab * pairs, 8 * slab * pairs),
                scaled, after(from_dev, start, *earlier), rho_re, rho_im,
            )

        if fresh:
            send3, keep3 = far_slab(3, start, from_dev)
            keep, send = project(send3)
        else:
            keep, send = project()
            send3, keep3 = far_slab(3, start, keep)
        got3 = exchange(send3, "dev", 1)
        total = keep + exchange(send, "grp", 1)
        send2, keep2 = slab_of(2, send3, total)
        got2 = exchange(send2, "dev", 1)
        total = total + exchange(total, "col", 1)
        sum3 = keep3 + after(got3, total)
        across = exchange(sum3, "col", 1)
        send1, keep1 = slab_of(1, send2, total, sum3)
        got1 = exchange(send1, "dev", 1)
        total = total + after(exchange(total, "grp", 2), send1)
        sum2 = keep2 + got2 + across
        far = exchange(sum2, "col", 2)
        send0, keep0 = slab_of(0, send1, total)
        total = total + after(exchange(total, "col", 2), send0)
        other = exchange(total, "grp", 1)
        sum1 = keep1 + after(got1, send0)
        near = exchange(sum1, "col", 1)
        send0, keep0 = small(
            functools.partial(spread_kernel, width), "spread", scalars, [shaped(panel_rows, half)] * 2,
            [pltpu.VMEM((panel_rows, pairs), jnp.float32)],
            (3 * 4 * panel_rows * slab * pairs, 8 * slab * pairs),
            total, after(other, sum1), weight, rho_re, rho_im, send0, keep0,
        )
        got0 = exchange(send0, "dev", 1)
        mine = keep0 + far
        mine = mine + after(near, mine)
        return mine, after(got0, mine)

    blocks = {}
    mine, by_dev = image(scaled, blocks)
    pulled = scale * (mine + by_dev)
    real_part = bare + damping * (bare + pulled[:width] - bare)
    imag_part = damping * pulled[width:]
    iterate = jnp.concatenate([real_part, imag_part], axis=0)
    for sweep in range(1, ITERS):
        mine, by_dev = image(scale * iterate, blocks)
    return small(
        functools.partial(end_kernel, width), "end", scalars, [shaped(half, width)] * 2,
        [], (0, 4 * 8 * half * panel_rows),
        mine, by_dev, iterate, bare, scale,
    )


def solution(mesh):
    placed = (
        P(("grp", "col"), "dev"),
        P(("grp", "col"), "dev"),
        P(("grp", "col", "dev")),
        P(None, None, "col", "dev", "grp"),
        P(("grp", "col", "dev"), None),
        P("dev"),
        P("dev"),
        P(),
        P(),
    )

    def shards(*blocks):
        half, width = blocks[4].shape
        pairs = blocks[0].shape[1]
        paired = mesh.shape["grp"] == 4 and mesh.shape["col"] == 4 and mesh.shape["dev"] == 2
        tiled = half % 128 == 0 and width % 128 == 0 and pairs % 128 == 0
        return (exchanged if paired and tiled and ITERS == 2 else general)(*blocks)

    return jax.shard_map(
        shards,
        mesh=mesh,
        in_specs=placed,
        out_specs=(P(("grp", "col", "dev"), None), P(("grp", "col", "dev"), None)),
        check_vma=False,
    )
```
